32 devices in a mesh: seq: 4 (over y, x), exp: 8 (over z, core).
Axes of the slice: x: 2, y: 2, z: 4, core: 2. Of those that a mesh axis runs over, the one named last changes fastest.
Arguments:
- tokens: bfloat16 [8192, 2048], P(('seq', 'exp')), may hold values from -128 to 128
- slot_embed: bfloat16 [2048, 64], P(None, 'exp'), may hold values from -0.397747564 to 0.397747564
- expert_in: bfloat16 [16, 2048, 4096], P('exp', None, 'seq'), may hold values from -0.125 to 0.125
- expert_out: bfloat16 [16, 4096, 2048], P('exp', 'seq'), may hold values from -0.09375 to 0.09375
- out_grad: bfloat16 [8192, 2048], P(('seq', 'exp')), may hold values from -0.59765625 to 0.59765625
Outputs:
- tok_grad: bfloat16 [8192, 2048], P(('seq', 'exp'))
- slot_grad: float32 [2048, 64], P('seq', 'exp')
The draws below stay inside these ranges and needn't reach their ends.
All inputs are finite; a program needn't handle non-finite values.
Results may differ from the reference program's by a relative error of at most 0.024.
Values may be sent and summed in bfloat16 or wider, within the bound.
No kernel may reach another device: no remote copies, remote signals or barrier semaphores. Data moves between devices by JAX's collectives and lax.ppermute only.
A program may use at most 64 MiB of HBM per device.

```python
import math
from functools import partial
import jax
import jax.numpy as jnp
from jax import lax

D = 2048
H = 4096
SLOTS = 4
EXPERTS = 16
S = 64
TOKENS = 8192


def slot_values(key):
    normal_draw = jax.random.normal(jax.random.fold_in(key, 101), (D, S), jnp.float32)
    return jnp.clip(normal_draw, -6.0, 6.0) * (3.0 / math.sqrt(D))


def draw_slot_embed(key, part):
    return slot_values(key).astype(jnp.bfloat16)


def draw_tokens(key, part):
    values = jnp.clip(jax.random.normal(jax.random.fold_in(key, 202), (TOKENS, D), jnp.float32), -6.0, 6.0)
    return jnp.clip(values, -128.0, 128.0).astype(jnp.bfloat16)


def block_levels(key, extent, shards, least, high):
    loudness, own = 1.0, jax.random.fold_in(key, 6)
    for position, shards_of in shards:
        steps = jnp.exp(jax.random.uniform(jax.random.fold_in(own, position), (shards_of,), jnp.float32, least / len(shards), high / len(shards)))
        loudness = loudness * jnp.repeat(steps, extent[position] // shards_of).reshape([-1 if axis == position else 1 for axis in range(len(extent))])
    return loudness


def centred(key, dims, spread, bound, cuts=(), kind=jnp.bfloat16):
    entries = spread * jax.random.normal(key, dims, jnp.float32)
    if cuts:
        entries = entries * block_levels(key, dims, cuts, -0.22, 0.18)
    return jnp.clip(entries, -bound, bound).astype(kind)


def setup_inputs(seed: int = 0) -> dict:
    seeds = jax.random.split(jax.random.key(seed), 6)
    tokens = draw_tokens(jax.random.fold_in(seeds[5], 71), 0)
    slot_embed = draw_slot_embed(jax.random.fold_in(seeds[5], 71), 0)
    expert_in = centred(seeds[2], (EXPERTS, D, H), D ** -0.5, 0.125, ((0, 8), (2, 4)))
    expert_out = centred(seeds[3], (EXPERTS, H, D), H ** -0.5, 0.09375, ((0, 8), (1, 4)))
    out_grad = centred(seeds[4], (TOKENS, D), 0.1, 0.59765625, ((0, 32),))
    return dict(tokens=tokens, slot_embed=slot_embed, expert_in=expert_in, expert_out=expert_out, out_grad=out_grad)


def contract_rows(left, right):
    return lax.dot_general(left, right, (((0,), (0,)), ((), ())), preferred_element_type=jnp.float32)

def contract_cols(left, right):
    return lax.dot_general(left, right, (((1,), (1,)), ((), ())), preferred_element_type=jnp.float32)

def expert_forward(operands):
    slot_rows, weight_in, weight_out = operands
    pre_act = jnp.dot(slot_rows, weight_in, preferred_element_type=jnp.float32)
    hidden = jax.nn.gelu(pre_act, approximate=True).astype(jnp.bfloat16)
    return (pre_act, jnp.dot(hidden, weight_out, preferred_element_type=jnp.float32))

def expert_backward(operands):
    grad_rows, pre_act, weight_in, weight_out = operands
    hid_grad = contract_cols(grad_rows, weight_out)
    _, pullback = jax.vjp(partial(jax.nn.gelu, approximate=True), pre_act)
    act_grad = pullback(hid_grad)[0].astype(jnp.bfloat16)
    return contract_cols(act_grad, weight_in)

def reference(tokens, slot_embed, expert_in, expert_out, out_grad):
    logits = jnp.dot(tokens, slot_embed, preferred_element_type=jnp.float32)
    col_top = lax.optimization_barrier(jnp.max(logits, axis=0))
    exponent = jnp.exp(logits - col_top)
    dispatch = exponent / lax.optimization_barrier(jnp.sum(exponent, axis=0))
    dispatch_b = dispatch.astype(jnp.bfloat16)
    combine_w = jax.nn.softmax(logits, axis=1)
    combine_b = combine_w.astype(jnp.bfloat16)
    slot_sum = contract_rows(dispatch_b, tokens)
    slot_in = slot_sum.astype(jnp.bfloat16).reshape(EXPERTS, SLOTS, D)
    pre_act, slot_part = lax.map(expert_forward, (slot_in, expert_in, expert_out))
    slot_out = slot_part.astype(jnp.bfloat16).reshape(S, D)
    comb_grad = contract_cols(out_grad, slot_out)
    grad_out = contract_rows(combine_b, out_grad).astype(jnp.bfloat16).reshape(EXPERTS, SLOTS, D)
    in_part = lax.map(expert_backward, (grad_out, pre_act, expert_in, expert_out))
    grad_in = in_part.astype(jnp.bfloat16).reshape(S, D)
    disp_grad = contract_cols(tokens, grad_in)
    centre = lax.optimization_barrier(jnp.sum(dispatch_b.astype(jnp.float32) * disp_grad, axis=0))
    comb_mean = lax.optimization_barrier(jnp.sum(combine_w * comb_grad, axis=1, keepdims=True))
    logit_grad = dispatch * (disp_grad - centre) + combine_w * (comb_grad - comb_mean)
    logit_b = logit_grad.astype(jnp.bfloat16)
    tok_grad = jnp.dot(dispatch_b, grad_in, preferred_element_type=jnp.float32) + contract_cols(logit_b, slot_embed)
    slot_grad = contract_rows(tokens, logit_b)
    return (tok_grad.astype(jnp.bfloat16), slot_grad)
```

```python
from functools import partial

import jax
import jax.numpy as jnp
from jax import lax
from jax.sharding import PartitionSpec as P

LANES = 128


def contract_cols(left, right):
    return lax.dot_general(
        left, right, (((1,), (1,)), ((), ())), preferred_element_type=jnp.float32
    )


def contract_rows(left, right):
    return lax.dot_general(
        left, right, (((0,), (0,)), ((), ())), preferred_element_type=jnp.float32
    )


def swap(x, axis, bit):
    return lax.ppermute(x, axis, [(k, k ^ bit) for k in range(lax.axis_size(axis))])


def gather_bits(n):
    return [1 << k for k in reversed(range(n.bit_length() - 1))]


def scatter_bits(n):
    return [1 << k for k in range(n.bit_length() - 1)]


def gathered(x, axis):
    for bit in gather_bits(lax.axis_size(axis)):
        x = jnp.concatenate([x, swap(x, axis, bit)], axis=0)
    return x


def pieces(x):
    high = lax.reduce_precision(x, 8, 7)
    mid = lax.reduce_precision(x - high, 8, 7)
    low = x - high - mid
    return [p.astype(jnp.bfloat16) for p in (high, mid, low)]


def packed(columns):
    parts = [p for c in columns for p in pieces(c)]
    rows = parts[0].shape[0]
    lane = lax.broadcasted_iota(jnp.int32, (rows, LANES), 1)
    out = jnp.zeros((rows, LANES), jnp.bfloat16)
    for k, part in enumerate(parts):
        out = jnp.where(lane == k, part, out)
    return out


def unpacked(block, count):
    f = block.astype(jnp.float32)
    return [
        f[:, 3 * k : 3 * k + 1] + f[:, 3 * k + 1 : 3 * k + 2] + f[:, 3 * k + 2 : 3 * k + 3]
        for k in range(count)
    ]


def merge(mine, other, width):
    top_a, total_a = unpacked(mine[:, 2 * width :], 2)
    top_b, total_b = unpacked(other[:, 2 * width :], 2)
    top = jnp.maximum(top_a, top_b)
    scale_a, scale_b = jnp.exp(top_a - top), jnp.exp(top_b - top)
    a, b = mine.astype(jnp.float32), other.astype(jnp.float32)
    sums = a[:, :width] * scale_a + b[:, :width] * scale_b
    grads = a[:, width : 2 * width] + b[:, width : 2 * width]
    return sums, grads, top, total_a * scale_a + total_b * scale_b


def message(sums, grads, top, total):
    return jnp.concatenate(
        [sums.astype(jnp.bfloat16), grads.astype(jnp.bfloat16), packed([top, total])], axis=1
    )


def shards(tokens, slot_embed, expert_in, expert_out, out_grad):
    experts_here = expert_in.shape[0]
    width = tokens.shape[1]
    n_exp, n_seq = lax.axis_size("exp"), lax.axis_size("seq")
    own = slot_embed.shape[1]

    table = gathered(slot_embed.T, "exp")
    logits = contract_cols(table, tokens)
    top = jnp.max(logits, axis=1, keepdims=True)
    weight = jnp.exp(logits - top)
    total = jnp.sum(weight, axis=1, keepdims=True)
    combine = jax.nn.softmax(logits, axis=0)
    sums = jnp.dot(weight.astype(jnp.bfloat16), tokens, preferred_element_type=jnp.float32)
    grads = jnp.dot(combine.astype(jnp.bfloat16), out_grad, preferred_element_type=jnp.float32)

    state = (sums, grads, top, total)
    for bit in scatter_bits(n_exp):
        packet = message(*state)
        half = packet.shape[0] // 2
        state = merge(packet[:half], swap(packet[half:], "exp", bit), width)
    for bit in scatter_bits(n_seq):
        packet = message(*state)
        state = merge(packet, swap(packet, "seq", bit), width)
    sums, grads, top, total = state
    slot_sum = sums / total

    slot_in = slot_sum.astype(jnp.bfloat16).reshape(experts_here, -1, width)
    pre_act = jnp.einsum("esd,edh->esh", slot_in, expert_in, preferred_element_type=jnp.float32)
    hidden = jax.nn.gelu(pre_act, approximate=True).astype(jnp.bfloat16)
    out_part = jnp.einsum("esh,ehd->esd", hidden, expert_out, preferred_element_type=jnp.float32)
    grad_out = grads.astype(jnp.bfloat16).reshape(experts_here, -1, width)
    hid_grad = jnp.einsum("esd,ehd->esh", grad_out, expert_out, preferred_element_type=jnp.float32)
    _, pullback = jax.vjp(partial(jax.nn.gelu, approximate=True), pre_act)
    act_grad = pullback(hid_grad)[0].astype(jnp.bfloat16)
    in_part = jnp.einsum("esh,edh->esd", act_grad, expert_in, preferred_element_type=jnp.float32)

    both = jnp.concatenate([out_part.reshape(-1, width), in_part.reshape(-1, width)], axis=1)
    for bit in scatter_bits(n_seq):
        packet = both.astype(jnp.bfloat16)
        both = packet.astype(jnp.float32) + swap(packet, "seq", bit).astype(jnp.float32)
    both = both.astype(jnp.bfloat16)
    centre = jnp.sum(slot_sum * both[:, width:].astype(jnp.float32), axis=1, keepdims=True)
    packet = jnp.concatenate([both, packed([centre, top, total])], axis=1)
    packet = gathered(packet, "exp")
    slot_all, grad_all = packet[:, :width], packet[:, width : 2 * width]
    centre, top, total = unpacked(packet[:, 2 * width :], 3)

    comb_grad = contract_cols(slot_all, out_grad)
    disp_grad = contract_cols(grad_all, tokens)
    dispatch = jnp.exp(logits - top) / total
    comb_mean = jnp.sum(combine * comb_grad, axis=0, keepdims=True)
    logit_grad = dispatch * (disp_grad - centre) + combine * (comb_grad - comb_mean)
    logit_b = logit_grad.astype(jnp.bfloat16)

    part = jnp.dot(logit_b, tokens, preferred_element_type=jnp.float32)
    tok_grad = contract_rows(
        jnp.concatenate([dispatch.astype(jnp.bfloat16), logit_b], axis=0),
        jnp.concatenate([grad_all, table], axis=0),
    ).astype(jnp.bfloat16)

    part = part.astype(jnp.bfloat16)
    for bit in scatter_bits(n_exp):
        half = part.shape[0] // 2
        got = swap(part[half:], "exp", bit).astype(jnp.float32)
        part = (part[:half].astype(jnp.float32) + got).astype(jnp.bfloat16)
    me = lax.axis_index("seq")
    for bit in reversed(scatter_bits(n_seq)):
        half = part.shape[1] // 2
        upper = (me & bit) != 0
        low, high = part[:, :half], part[:, half:]
        got = swap(jnp.where(upper, low, high), "seq", bit).astype(jnp.float32)
        part = jnp.where(upper, high, low).astype(jnp.float32) + got
        if bit != 1:
            part = part.astype(jnp.bfloat16)
    return (tok_grad, part.T)


def solution(mesh):
    placed = (
        P(("seq", "exp"), None),
        P(None, "exp"),
        P("exp", None, "seq"),
        P("exp", "seq", None),
        P(("seq", "exp"), None),
    )
    return jax.shard_map(
        shards,
        mesh=mesh,
        in_specs=placed,
        out_specs=(P(("seq", "exp"), None), P("seq", "exp")),
        check_vma=False,
    )
```

```python
from functools import partial
import math

import jax
import jax.numpy as jnp
from jax import lax
from jax.experimental import pallas as pl
from jax.experimental.pallas import tpu as pltpu
from jax.sharding import PartitionSpec as P

LANES = 128
F32 = jnp.float32
BF16 = jnp.bfloat16
MIB = 1 << 20


def swap(x, axis, mask):
    return lax.ppermute(x, axis, [(k, k ^ mask) for k in range(lax.axis_size(axis))])


def swaps(parts, axis, masks):
    return [swap(x, axis, mask) for x, mask in zip(parts, masks)]


def groups(n, first):
    bits = [1 << k for k in range(n.bit_length() - 1) if 1 << k >= first]
    return [
        [b for b in (pair[0], *pair[1:], sum(pair)) if b]
        if len(pair) == 2
        else [pair[0]]
        for pair in (bits[k : k + 2] for k in range(0, len(bits), 2))
    ]


def in_vmem(x):
    return pltpu.with_memory_space_constraint(x, pltpu.VMEM)


def local_call(body, outs, *operands, limit=8, to_hbm=()):
    return pl.pallas_call(
        body,
        out_shape=tuple(
            jax.ShapeDtypeStruct(s, d) if k in to_hbm else pltpu.VMEM(s, d)
            for k, (s, d) in enumerate(outs)
        ),
        in_specs=[pl.BlockSpec(memory_space=pltpu.VMEM)] * len(operands),
        out_specs=tuple(pl.BlockSpec(memory_space=pltpu.VMEM) for _ in outs),
        compiler_params=pltpu.CompilerParams(vmem_limit_bytes=limit * MIB),
    )(*[in_vmem(x) for x in operands])


def product(left, right, over_left, over_right):
    return lax.dot_general(
        left, right, (((over_left,), (over_right,)), ((), ())), preferred_element_type=F32
    )


def rounded(x):
    return x.astype(BF16).astype(F32)


def packed(columns, rows):
    lane = lax.broadcasted_iota(jnp.int32, (rows, LANES), 1)
    out = jnp.zeros((rows, LANES), F32)
    for k, x in enumerate(columns):
        high = rounded(x)
        mid = rounded(x - high)
        for j, piece in enumerate((high, mid, x - high - mid)):
            out = jnp.where(lane == 3 * k + j, piece, out)
    return out


def unpacked(block, count):
    lane = lax.broadcasted_iota(jnp.int32, block.shape, 1)
    return [
        jnp.sum(
            jnp.where((lane >= 3 * k) & (lane < 3 * k + 3), block, 0.0), axis=1, keepdims=True
        )
        for k in range(count)
    ]


def concat_kernel(*refs):
    out = refs[-1]
    out[...] = jnp.concatenate([r[...].astype(F32) for r in refs[:-1]], axis=0).astype(BF16)


def stack(parts):
    if len(parts) == 1:
        return parts[0]
    rows = sum(p.shape[0] for p in parts)
    return local_call(concat_kernel, [((rows, parts[0].shape[1]), BF16)], *parts)[0]


def softmax_columns(logits):
    weight = jnp.exp(logits - jnp.max(logits, axis=0, keepdims=True))
    return weight / jnp.sum(weight, axis=0, keepdims=True)


def first_kernel(near, far, tokens, out_grad, logits_out, keep, send):
    width = tokens.shape[1]
    half = near.shape[0]
    logits = jnp.concatenate(
        [product(near[...], tokens[...], 1, 1), product(far[...], tokens[...], 1, 1)], axis=0
    )
    logits_out[...] = logits
    top = jnp.max(logits, axis=1, keepdims=True)
    weight = jnp.exp(logits - top)
    stats = packed([top, jnp.sum(weight, axis=1, keepdims=True)], 2 * half).astype(BF16)
    sums = product(weight.astype(BF16), tokens[...], 1, 0).astype(BF16)
    grads = product(softmax_columns(logits).astype(BF16), out_grad[...], 1, 0).astype(BF16)
    for k, out in enumerate((keep, send)):
        rows = slice(k * half, (k + 1) * half)
        out[:, :width] = sums[rows]
        out[:, width : 2 * width] = grads[rows]
        out[:, 2 * width :] = stats[rows]


def merged(refs, width):
    stats = [unpacked(r[:, 2 * width :].astype(F32), 2) for r in refs]
    top = stats[0][0]
    for other, _ in stats[1:]:
        top = jnp.maximum(top, other)
    scales = [jnp.exp(t - top) for t, _ in stats]
    total = sum(s * l for s, (_, l) in zip(scales, stats))
    sums = sum(s * r[:, :width].astype(F32) for s, r in zip(scales, refs))
    grads = sum(r[:, width : 2 * width].astype(F32) for r in refs)
    return sums, grads, top, total


def merge_kernel(count, width, *refs):
    sums, grads, top, total = merged(refs[:count], width)
    outs = refs[count:]
    rows = outs[0].shape[0]
    stats = packed([top, total], sums.shape[0])
    for k, out in enumerate(outs):
        part = slice(k * rows, (k + 1) * rows)
        out[:, :width] = sums[part].astype(BF16)
        out[:, width : 2 * width] = grads[part].astype(BF16)
        out[:, 2 * width :] = stats[part].astype(BF16)


def merge(parts, width, pieces):
    rows, columns = parts[0].shape
    return local_call(
        partial(merge_kernel, len(parts), width),
        [((rows // pieces, columns), BF16)] * pieces,
        *parts,
    )


def gelu_and_slope(v):
    root = math.sqrt(2.0 / math.pi)
    t = jnp.tanh(root * (v + 0.044715 * (v * v * v)))
    slope = 0.5 * (1.0 + t) + 0.5 * v * (1.0 - t * t) * (root * (1.0 + 3 * 0.044715 * (v * v)))
    return 0.5 * v * (1.0 + t), slope


def expert_kernel(count, width, *refs):
    parts = refs[:count]
    weight_in, weight_out, both, slot_sum, stats = refs[count:]
    sums, grads, top, total = merged(parts, width)
    stats[...] = packed([top, total], stats.shape[0])
    sums = sums / total
    slot_sum[...] = sums
    slot_in, grad_out = sums.astype(BF16), grads.astype(BF16)
    experts, _, units = weight_in.shape
    rows = sums.shape[0]
    step = min(units, 512)
    row = lax.broadcasted_iota(jnp.int32, (rows, step), 0)
    out_part = jnp.zeros((rows, width), F32)
    in_part = jnp.zeros((rows, width), F32)
    for e in range(experts):
        own = (row >= e * (rows // experts)) & (row < (e + 1) * (rows // experts))
        for c in range(units // step):
            at = slice(c * step, (c + 1) * step)
            pre_act = product(slot_in, weight_in[e, :, at], 1, 0)
            hid_grad = product(grad_out, weight_out[e, at, :], 1, 1)
            act, slope = gelu_and_slope(pre_act)
            hidden = jnp.where(own, act, 0.0).astype(BF16)
            act_grad = jnp.where(own, hid_grad * slope, 0.0).astype(BF16)
            out_part += product(hidden, weight_out[e, at, :], 1, 0)
            in_part += product(act_grad, weight_in[e, :, at], 1, 1)
    both[:, :width] = out_part.astype(BF16)
    both[:, width:] = in_part.astype(BF16)


def sum_kernel(count, *refs):
    total = sum(r[...].astype(F32) for r in refs[:count])
    outs = refs[count:]
    rows = outs[0].shape[0]
    for k, out in enumerate(outs):
        out[...] = total[k * rows : (k + 1) * rows].astype(out.dtype)


def sum_of(parts, pieces, dtype):
    rows, columns = parts[0].shape
    return local_call(
        partial(sum_kernel, len(parts)), [((rows // pieces, columns), dtype)] * pieces, *parts
    )


def centre_kernel(count, width, *refs):
    parts = refs[:count]
    slot_sum, stats, out = refs[count:]
    total = sum(r[...].astype(F32) for r in parts).astype(BF16)
    grad_in = total[:, width:].astype(F32)
    centre = jnp.sum(slot_sum[...] * grad_in, axis=1, keepdims=True)
    top, denominator = unpacked(stats[...], 2)
    out[:, : 2 * width] = total
    out[:, 2 * width :] = packed([centre, top, denominator], stats.shape[0]).astype(BF16)


def second_kernel(near, far, logits, tokens, out_grad, weights, keep, send):
    width = tokens.shape[1]
    half = near.shape[0]

    def against(columns, rows):
        return jnp.concatenate(
            [product(x[:, columns], rows[...], 1, 1) for x in (near, far)], axis=0
        )

    comb_grad = against(slice(0, width), out_grad)
    disp_grad = against(slice(width, 2 * width), tokens)
    stats = jnp.concatenate([x[:, 2 * width :].astype(F32) for x in (near, far)], axis=0)
    centre, top, total = unpacked(stats, 3)
    scores = logits[...]
    dispatch = jnp.exp(scores - top) / total
    combine = softmax_columns(scores)
    comb_mean = jnp.sum(combine * comb_grad, axis=0, keepdims=True)
    logit_grad = dispatch * (disp_grad - centre) + combine * (comb_grad - comb_mean)
    logit_b = logit_grad.astype(BF16)
    weights[: 2 * half] = dispatch.astype(BF16)
    weights[2 * half :] = logit_b
    part = product(logit_b, tokens[...], 1, 0).astype(BF16)
    keep[...] = part[:half]
    send[...] = part[half:]


def patch_kernel(weights, near, far, table_near, table_far, out):
    width = out.shape[1]
    rows = jnp.concatenate(
        [x[:, width : 2 * width] for x in (near, far)] + [table_near[...], table_far[...]], axis=0
    )
    out[...] = product(weights[...], rows, 0, 0).astype(BF16)


def shards(tokens, slot_embed, expert_in, expert_out, out_grad):
    width = tokens.shape[1]
    patches = tokens.shape[0]
    own = slot_embed.shape[1]
    n_exp, n_seq = lax.axis_size("exp"), lax.axis_size("seq")
    slots = own * n_exp
    half = slots // 2
    columns = 2 * width + LANES
    chip_groups = groups(n_exp, 2)
    seq_groups = groups(n_seq, 1)

    def gathered_over_chips(x):
        for masks in reversed(chip_groups):
            x = stack([x] + swaps([x] * len(masks), "exp", masks))
        return x

    table_near = gathered_over_chips(slot_embed.T)
    table_far = swap(table_near, "exp", 1)

    logits, keep, send = local_call(
        first_kernel,
        [((slots, patches), F32), ((half, columns), BF16), ((half, columns), BF16)],
        table_near,
        table_far,
        tokens,
        out_grad,
        limit=12,
    )
    parts = [keep, swap(send, "exp", 1)]
    for masks in chip_groups:
        pieces = merge(parts, width, len(masks) + 1)
        parts = [pieces[0]] + swaps(pieces[1:], "exp", masks)
    for masks in seq_groups:
        (x,) = merge(parts, width, 1)
        parts = [x] + swaps([x] * len(masks), "seq", masks)

    both, slot_sum, stats = local_call(
        partial(expert_kernel, len(parts), width),
        [((own, 2 * width), BF16), ((own, width), F32), ((own, LANES), F32)],
        *parts,
        expert_in,
        expert_out,
        limit=16,
    )
    parts = [both]
    for k, masks in enumerate(seq_groups):
        if k:
            parts = list(sum_of(parts, 1, BF16))
        parts = parts + swaps(parts * len(masks), "seq", masks)
    (packet,) = local_call(
        partial(centre_kernel, len(parts), width),
        [((own, columns), BF16)],
        *parts,
        slot_sum,
        stats,
    )
    near = gathered_over_chips(packet)
    far = swap(near, "exp", 1)

    weights, keep, send = local_call(
        second_kernel,
        [((2 * slots, patches), BF16), ((half, width), BF16), ((half, width), BF16)],
        near,
        far,
        logits,
        tokens,
        out_grad,
        limit=12,
    )
    (tok_grad,) = local_call(
        patch_kernel,
        [((patches, width), BF16)],
        weights,
        near,
        far,
        table_near,
        table_far,
        limit=12,
        to_hbm=(0,),
    )

    parts = [keep, swap(send, "exp", 1)]
    for masks in chip_groups:
        pieces = sum_of(parts, len(masks) + 1, BF16)
        parts = [pieces[0]] + swaps(pieces[1:], "exp", masks)
    part = sum(p.astype(F32) for p in parts)
    me = lax.axis_index("seq")
    share = width // n_seq
    for masks in reversed(seq_groups):
        base = me & (min(masks) - 1)
        count = len(masks) + 1
        span = part.shape[1] // count
        low = min(masks)
        mine = (me // low) % count

        def block(mask):
            at = mine ^ (mask // low)
            return lax.dynamic_slice_in_dim(part, at * span, span, axis=1)

        part = block(0) + sum(
            swap(block(mask).astype(BF16), "seq", mask).astype(F32) for mask in masks
        )
    return (tok_grad, part.T)


def solution(mesh):
    placed = (
        P(("seq", "exp"), None),
        P(None, "exp"),
        P("exp", None, "seq"),
        P("exp", "seq", None),
        P(("seq", "exp"), None),
    )
    return jax.shard_map(
        shards,
        mesh=mesh,
        in_specs=placed,
        out_specs=(P(("seq", "exp"), None), P("seq", "exp")),
        check_vma=False,
    )
```

```python
from functools import partial
import math

import jax
import jax.numpy as jnp
from jax import lax
from jax.experimental import pallas as pl
from jax.experimental.pallas import tpu as pltpu
from jax.sharding import PartitionSpec as P

LANES = 128
F32 = jnp.float32
BF16 = jnp.bfloat16
MIB = 1 << 20


def swap(x, axis, mask):
    return lax.ppermute(x, axis, [(k, k ^ mask) for k in range(lax.axis_size(axis))])


def swaps(parts, axis, masks):
    return [swap(x, axis, mask) for x, mask in zip(parts, masks)]


def groups(n, first):
    bits = [1 << k for k in range(n.bit_length() - 1) if 1 << k >= first]
    return [
        [b for b in (pair[0], *pair[1:], sum(pair)) if b]
        if len(pair) == 2
        else [pair[0]]
        for pair in (bits[k : k + 2] for k in range(0, len(bits), 2))
    ]


def in_vmem(x):
    return pltpu.with_memory_space_constraint(x, pltpu.VMEM)


def local_call(body, outs, *operands, limit=8, to_hbm=()):
    return pl.pallas_call(
        body,
        out_shape=tuple(
            jax.ShapeDtypeStruct(s, d) if k in to_hbm else pltpu.VMEM(s, d)
            for k, (s, d) in enumerate(outs)
        ),
        in_specs=[pl.BlockSpec(memory_space=pltpu.VMEM)] * len(operands),
        out_specs=tuple(pl.BlockSpec(memory_space=pltpu.VMEM) for _ in outs),
        compiler_params=pltpu.CompilerParams(vmem_limit_bytes=limit * MIB),
        cost_estimate=pl.CostEstimate(flops=10**10, bytes_accessed=4 * MIB, transcendentals=0),
    )(*[in_vmem(x) for x in operands])


def product(left, right, over_left, over_right):
    return lax.dot_general(
        left, right, (((over_left,), (over_right,)), ((), ())), preferred_element_type=F32
    )


def rounded(x):
    return x.astype(BF16).astype(F32)


def packed(columns, rows):
    lane = lax.broadcasted_iota(jnp.int32, (rows, LANES), 1)
    out = jnp.zeros((rows, LANES), F32)
    for k, x in enumerate(columns):
        high = rounded(x)
        mid = rounded(x - high)
        for j, piece in enumerate((high, mid, x - high - mid)):
            out = jnp.where(lane == 3 * k + j, piece, out)
    return out


def unpacked(block, count):
    lane = lax.broadcasted_iota(jnp.int32, block.shape, 1)
    return [
        jnp.sum(
            jnp.where((lane >= 3 * k) & (lane < 3 * k + 3), block, 0.0), axis=1, keepdims=True
        )
        for k in range(count)
    ]


def load_kernel(source, out, semaphore):
    copy = pltpu.make_async_copy(source, out, semaphore)
    copy.start()
    copy.wait()


def loaded(x):
    return pl.pallas_call(
        load_kernel,
        out_shape=pltpu.VMEM(x.shape, x.dtype),
        in_specs=[pl.BlockSpec(memory_space=pl.ANY)],
        out_specs=pl.BlockSpec(memory_space=pltpu.VMEM),
        scratch_shapes=[pltpu.SemaphoreType.DMA],
        compiler_params=pltpu.CompilerParams(vmem_limit_bytes=2 * MIB),
        cost_estimate=pl.CostEstimate(flops=10**9, bytes_accessed=2 * x.size, transcendentals=0),
    )(x)


def concat_kernel(*refs):
    out = refs[-1]
    out[...] = jnp.concatenate([r[...].astype(F32) for r in refs[:-1]], axis=0).astype(BF16)


def stack(parts):
    if len(parts) == 1:
        return parts[0]
    rows = sum(p.shape[0] for p in parts)
    return local_call(concat_kernel, [((rows, parts[0].shape[1]), BF16)], *parts)[0]


def softmax_columns(logits):
    weight = jnp.exp(logits - jnp.max(logits, axis=0, keepdims=True))
    return weight / jnp.sum(weight, axis=0, keepdims=True)


def first_kernel(near, far, tokens, out_grad, logits_out, keep, send):
    width = tokens.shape[1]
    half = near.shape[0]
    logits = jnp.concatenate(
        [product(near[...], tokens[...], 1, 1), product(far[...], tokens[...], 1, 1)], axis=0
    )
    logits_out[...] = logits
    top = jnp.max(logits, axis=1, keepdims=True)
    weight = jnp.exp(logits - top)
    stats = packed([top, jnp.sum(weight, axis=1, keepdims=True)], 2 * half).astype(BF16)
    sums = product(weight.astype(BF16), tokens[...], 1, 0).astype(BF16)
    grads = product(softmax_columns(logits).astype(BF16), out_grad[...], 1, 0).astype(BF16)
    for k, out in enumerate((keep, send)):
        rows = slice(k * half, (k + 1) * half)
        out[:, :width] = sums[rows]
        out[:, width : 2 * width] = grads[rows]
        out[:, 2 * width :] = stats[rows]


def merged(refs, width):
    stats = [unpacked(r[:, 2 * width :].astype(F32), 2) for r in refs]
    top = stats[0][0]
    for other, _ in stats[1:]:
        top = jnp.maximum(top, other)
    scales = [jnp.exp(t - top) for t, _ in stats]
    total = sum(s * l for s, (_, l) in zip(scales, stats))
    sums = sum(s * r[:, :width].astype(F32) for s, r in zip(scales, refs))
    grads = sum(r[:, width : 2 * width].astype(F32) for r in refs)
    return sums, grads, top, total


def merge_kernel(count, width, *refs):
    sums, grads, top, total = merged(refs[:count], width)
    outs = refs[count:]
    rows = outs[0].shape[0]
    stats = packed([top, total], sums.shape[0])
    for k, out in enumerate(outs):
        part = slice(k * rows, (k + 1) * rows)
        out[:, :width] = sums[part].astype(BF16)
        out[:, width : 2 * width] = grads[part].astype(BF16)
        out[:, 2 * width :] = stats[part].astype(BF16)


def merge(parts, width, pieces):
    rows, columns = parts[0].shape
    return local_call(
        partial(merge_kernel, len(parts), width),
        [((rows // pieces, columns), BF16)] * pieces,
        *parts,
    )


def gelu_and_slope(v):
    root = math.sqrt(2.0 / math.pi)
    t = jnp.tanh(root * (v + 0.044715 * (v * v * v)))
    slope = 0.5 * (1.0 + t) + 0.5 * v * (1.0 - t * t) * (root * (1.0 + 3 * 0.044715 * (v * v)))
    return 0.5 * v * (1.0 + t), slope


def expert_kernel(count, width, *refs):
    parts = refs[:count]
    weight_in, weight_out, both, slot_sum, stats = refs[count:]
    sums, grads, top, total = merged(parts, width)
    stats[...] = packed([top, total], stats.shape[0])
    sums = sums / total
    slot_sum[...] = sums
    slot_in, grad_out = sums.astype(BF16), grads.astype(BF16)
    experts, _, units = weight_in.shape
    rows = sums.shape[0]
    step = min(units, 512)
    row = lax.broadcasted_iota(jnp.int32, (rows, step), 0)
    out_part = jnp.zeros((rows, width), F32)
    in_part = jnp.zeros((rows, width), F32)
    for e in range(experts):
        own = (row >= e * (rows // experts)) & (row < (e + 1) * (rows // experts))
        for c in range(units // step):
            at = slice(c * step, (c + 1) * step)
            pre_act = product(slot_in, weight_in[e, :, at], 1, 0)
            hid_grad = product(grad_out, weight_out[e, at, :], 1, 1)
            act, slope = gelu_and_slope(pre_act)
            hidden = jnp.where(own, act, 0.0).astype(BF16)
            act_grad = jnp.where(own, hid_grad * slope, 0.0).astype(BF16)
            out_part += product(hidden, weight_out[e, at, :], 1, 0)
            in_part += product(act_grad, weight_in[e, :, at], 1, 1)
    both[:, :width] = out_part.astype(BF16)
    both[:, width:] = in_part.astype(BF16)


def sum_kernel(count, *refs):
    total = sum(r[...].astype(F32) for r in refs[:count])
    outs = refs[count:]
    rows = outs[0].shape[0]
    for k, out in enumerate(outs):
        out[...] = total[k * rows : (k + 1) * rows].astype(out.dtype)


def sum_of(parts, pieces, dtype):
    rows, columns = parts[0].shape
    return local_call(
        partial(sum_kernel, len(parts)), [((rows // pieces, columns), dtype)] * pieces, *parts
    )


def centre_kernel(count, width, *refs):
    parts = refs[:count]
    slot_sum, stats, out = refs[count:]
    total = sum(r[...].astype(F32) for r in parts).astype(BF16)
    grad_in = total[:, width:].astype(F32)
    centre = jnp.sum(slot_sum[...] * grad_in, axis=1, keepdims=True)
    top, denominator = unpacked(stats[...], 2)
    out[:, : 2 * width] = total
    out[:, 2 * width :] = packed([centre, top, denominator], stats.shape[0]).astype(BF16)


def second_kernel(near, far, logits, tokens, out_grad, weights, keep, send):
    width = tokens.shape[1]
    half = near.shape[0]

    def against(columns, rows):
        return jnp.concatenate(
            [product(x[:, columns], rows[...], 1, 1) for x in (near, far)], axis=0
        )

    comb_grad = against(slice(0, width), out_grad)
    disp_grad = against(slice(width, 2 * width), tokens)
    stats = jnp.concatenate([x[:, 2 * width :].astype(F32) for x in (near, far)], axis=0)
    centre, top, total = unpacked(stats, 3)
    scores = logits[...]
    dispatch = jnp.exp(scores - top) / total
    combine = softmax_columns(scores)
    comb_mean = jnp.sum(combine * comb_grad, axis=0, keepdims=True)
    logit_grad = dispatch * (disp_grad - centre) + combine * (comb_grad - comb_mean)
    logit_b = logit_grad.astype(BF16)
    weights[: 2 * half] = dispatch.astype(BF16)
    weights[2 * half :] = logit_b
    part = product(logit_b, tokens[...], 1, 0).astype(BF16)
    keep[...] = part[:half]
    send[...] = part[half:]


def patch_kernel(weights, near, far, table_near, table_far, out):
    width = out.shape[1]
    rows = jnp.concatenate(
        [x[:, width : 2 * width] for x in (near, far)] + [table_near[...], table_far[...]], axis=0
    )
    out[...] = product(weights[...], rows, 0, 0).astype(BF16)


def shards(tokens, slot_embed, expert_in, expert_out, out_grad):
    width = tokens.shape[1]
    patches = tokens.shape[0]
    own = slot_embed.shape[1]
    n_exp, n_seq = lax.axis_size("exp"), lax.axis_size("seq")
    slots = own * n_exp
    half = slots // 2
    columns = 2 * width + LANES
    chip_groups = groups(n_exp, 2)
    seq_groups = groups(n_seq, 1)

    def gathered_over_chips(x, here):
        for masks in reversed(chip_groups):
            x = here = stack([here] + swaps([x] * len(masks), "exp", masks))
        return x

    table_near = gathered_over_chips(slot_embed.T, loaded(slot_embed.T))
    table_far = swap(table_near, "exp", 1)

    logits, keep, send = local_call(
        first_kernel,
        [((slots, patches), F32), ((half, columns), BF16), ((half, columns), BF16)],
        table_near,
        table_far,
        tokens,
        out_grad,
        limit=12,
    )
    parts = [keep, swap(send, "exp", 1)]
    for masks in chip_groups:
        pieces = merge(parts, width, len(masks) + 1)
        parts = [pieces[0]] + swaps(pieces[1:], "exp", masks)
    for masks in seq_groups:
        (x,) = merge(parts, width, 1)
        parts = [x] + swaps([x] * len(masks), "seq", masks)

    both, slot_sum, stats = local_call(
        partial(expert_kernel, len(parts), width),
        [((own, 2 * width), BF16), ((own, width), F32), ((own, LANES), F32)],
        *parts,
        expert_in,
        expert_out,
        limit=16,
    )
    parts = [both]
    for k, masks in enumerate(seq_groups):
        if k:
            parts = list(sum_of(parts, 1, BF16))
        parts = parts + swaps(parts * len(masks), "seq", masks)
    (packet,) = local_call(
        partial(centre_kernel, len(parts), width),
        [((own, columns), BF16)],
        *parts,
        slot_sum,
        stats,
    )
    near = gathered_over_chips(packet, packet)
    far = swap(near, "exp", 1)

    weights, keep, send = local_call(
        second_kernel,
        [((2 * slots, patches), BF16), ((half, width), BF16), ((half, width), BF16)],
        near,
        far,
        logits,
        tokens,
        out_grad,
        limit=12,
    )
    (tok_grad,) = local_call(
        patch_kernel,
        [((patches, width), BF16)],
        weights,
        near,
        far,
        table_near,
        table_far,
        limit=12,
        to_hbm=(0,),
    )

    parts = [keep, swap(send, "exp", 1)]
    for masks in chip_groups:
        pieces = sum_of(parts, len(masks) + 1, BF16)
        parts = [pieces[0]] + swaps(pieces[1:], "exp", masks)
    part = sum(p.astype(F32) for p in parts)
    me = lax.axis_index("seq")
    share = width // n_seq
    for masks in reversed(seq_groups):
        base = me & (min(masks) - 1)
        count = len(masks) + 1
        span = part.shape[1] // count
        low = min(masks)
        mine = (me // low) % count

        def block(mask):
            at = mine ^ (mask // low)
            return lax.dynamic_slice_in_dim(part, at * span, span, axis=1)

        part = block(0) + sum(
            swap(block(mask).astype(BF16), "seq", mask).astype(F32) for mask in masks
        )
    return (tok_grad, part.T)


def solution(mesh):
    placed = (
        P(("seq", "exp"), None),
        P(None, "exp"),
        P("exp", None, "seq"),
        P("exp", "seq", None),
        P(("seq", "exp"), None),
    )
    return jax.shard_map(
        shards,
        mesh=mesh,
        in_specs=placed,
        out_specs=(P(("seq", "exp"), None), P("seq", "exp")),
        check_vma=False,
    )
```

```python
from functools import partial
import math

import jax
import jax.numpy as jnp
from jax import lax
from jax.experimental import pallas as pl
from jax.experimental.pallas import tpu as pltpu
from jax.sharding import PartitionSpec as P

LANES = 128
F32 = jnp.float32
BF16 = jnp.bfloat16
MIB = 1 << 20


def swap(x, axis, mask):
    return lax.ppermute(x, axis, [(k, k ^ mask) for k in range(lax.axis_size(axis))])


def swaps(parts, axis, masks):
    return [swap(x, axis, mask) for x, mask in zip(parts, masks)]


def groups(n, first):
    bits = [1 << k for k in range(n.bit_length() - 1) if 1 << k >= first]
    return [
        [b for b in (pair[0], *pair[1:], sum(pair)) if b]
        if len(pair) == 2
        else [pair[0]]
        for pair in (bits[k : k + 2] for k in range(0, len(bits), 2))
    ]


def in_vmem(x):
    return pltpu.with_memory_space_constraint(x, pltpu.VMEM)


def local_call(body, outs, *operands, limit=8, to_hbm=()):
    return pl.pallas_call(
        body,
        out_shape=tuple(
            jax.ShapeDtypeStruct(s, d) if k in to_hbm else pltpu.VMEM(s, d)
            for k, (s, d) in enumerate(outs)
        ),
        in_specs=[pl.BlockSpec(memory_space=pltpu.VMEM)] * len(operands),
        out_specs=tuple(pl.BlockSpec(memory_space=pltpu.VMEM) for _ in outs),
        compiler_params=pltpu.CompilerParams(vmem_limit_bytes=limit * MIB),
        cost_estimate=pl.CostEstimate(flops=10**10, bytes_accessed=4 * MIB, transcendentals=0),
    )(*[in_vmem(x) for x in operands])


def product(left, right, over_left, over_right):
    return lax.dot_general(
        left, right, (((over_left,), (over_right,)), ((), ())), preferred_element_type=F32
    )


def rounded(x):
    return x.astype(BF16).astype(F32)


def packed(columns, rows):
    lane = lax.broadcasted_iota(jnp.int32, (rows, LANES), 1)
    out = jnp.zeros((rows, LANES), F32)
    for k, x in enumerate(columns):
        high = rounded(x)
        mid = rounded(x - high)
        for j, piece in enumerate((high, mid, x - high - mid)):
            out = jnp.where(lane == 3 * k + j, piece, out)
    return out


def unpacked(block, count):
    lane = lax.broadcasted_iota(jnp.int32, block.shape, 1)
    return [
        jnp.sum(
            jnp.where((lane >= 3 * k) & (lane < 3 * k + 3), block, 0.0), axis=1, keepdims=True
        )
        for k in range(count)
    ]


def load_kernel(source, out, semaphore):
    copy = pltpu.make_async_copy(source, out, semaphore)
    copy.start()
    copy.wait()


def loaded(x):
    return pl.pallas_call(
        load_kernel,
        out_shape=pltpu.VMEM(x.shape, x.dtype),
        in_specs=[pl.BlockSpec(memory_space=pl.ANY)],
        out_specs=pl.BlockSpec(memory_space=pltpu.VMEM),
        scratch_shapes=[pltpu.SemaphoreType.DMA],
        compiler_params=pltpu.CompilerParams(vmem_limit_bytes=2 * MIB),
        cost_estimate=pl.CostEstimate(flops=10**9, bytes_accessed=2 * x.size, transcendentals=0),
    )(x)


def concat_kernel(*refs):
    out = refs[-1]
    out[...] = jnp.concatenate([r[...].astype(F32) for r in refs[:-1]], axis=0).astype(BF16)


def stack(parts):
    if len(parts) == 1:
        return parts[0]
    rows = sum(p.shape[0] for p in parts)
    return local_call(concat_kernel, [((rows, parts[0].shape[1]), BF16)], *parts)[0]


def softmax_columns(logits):
    weight = jnp.exp(logits - jnp.max(logits, axis=0, keepdims=True))
    return weight / jnp.sum(weight, axis=0, keepdims=True)


def first_kernel(near, far, tokens, out_grad, logits_out, keep, send):
    width = tokens.shape[1]
    half = near.shape[0]
    logits = jnp.concatenate(
        [product(near[...], tokens[...], 1, 1), product(far[...], tokens[...], 1, 1)], axis=0
    )
    logits_out[...] = logits
    top = jnp.max(logits, axis=1, keepdims=True)
    weight = jnp.exp(logits - top)
    stats = packed([top, jnp.sum(weight, axis=1, keepdims=True)], 2 * half).astype(BF16)
    sums = product(weight.astype(BF16), tokens[...], 1, 0).astype(BF16)
    grads = product(softmax_columns(logits).astype(BF16), out_grad[...], 1, 0).astype(BF16)
    for k, out in enumerate((keep, send)):
        rows = slice(k * half, (k + 1) * half)
        out[:, :width] = sums[rows]
        out[:, width : 2 * width] = grads[rows]
        out[:, 2 * width :] = stats[rows]


def merged(refs, width):
    stats = [unpacked(r[:, 2 * width :].astype(F32), 2) for r in refs]
    top = stats[0][0]
    for other, _ in stats[1:]:
        top = jnp.maximum(top, other)
    scales = [jnp.exp(t - top) for t, _ in stats]
    total = sum(s * l for s, (_, l) in zip(scales, stats))
    sums = sum(s * r[:, :width].astype(F32) for s, r in zip(scales, refs))
    grads = sum(r[:, width : 2 * width].astype(F32) for r in refs)
    return sums, grads, top, total


def merge_kernel(count, width, *refs):
    sums, grads, top, total = merged(refs[:count], width)
    outs = refs[count:]
    rows = outs[0].shape[0]
    stats = packed([top, total], sums.shape[0])
    for k, out in enumerate(outs):
        part = slice(k * rows, (k + 1) * rows)
        out[:, :width] = sums[part].astype(BF16)
        out[:, width : 2 * width] = grads[part].astype(BF16)
        out[:, 2 * width :] = stats[part].astype(BF16)


def merge(parts, width, pieces):
    rows, columns = parts[0].shape
    return local_call(
        partial(merge_kernel, len(parts), width),
        [((rows // pieces, columns), BF16)] * pieces,
        *parts,
    )


def gelu_and_slope(v):
    root = math.sqrt(2.0 / math.pi)
    t = jnp.tanh(root * (v + 0.044715 * (v * v * v)))
    slope = 0.5 * (1.0 + t) + 0.5 * v * (1.0 - t * t) * (root * (1.0 + 3 * 0.044715 * (v * v)))
    return 0.5 * v * (1.0 + t), slope


def expert_kernel(count, width, *refs):
    parts = refs[:count]
    weight_in, weight_out, both, slot_sum, stats = refs[count:]
    sums, grads, top, total = merged(parts, width)
    stats[...] = packed([top, total], stats.shape[0])
    sums = sums / total
    slot_sum[...] = sums
    slot_in, grad_out = sums.astype(BF16), grads.astype(BF16)
    experts, _, units = weight_in.shape
    rows = sums.shape[0]
    step = min(units, 512)
    row = lax.broadcasted_iota(jnp.int32, (rows, step), 0)
    out_part = jnp.zeros((rows, width), F32)
    in_part = jnp.zeros((rows, width), F32)
    for e in range(experts):
        own = (row >= e * (rows // experts)) & (row < (e + 1) * (rows // experts))
        for c in range(units // step):
            at = slice(c * step, (c + 1) * step)
            pre_act = product(slot_in, weight_in[e, :, at], 1, 0)
            hid_grad = product(grad_out, weight_out[e, at, :], 1, 1)
            act, slope = gelu_and_slope(pre_act)
            hidden = jnp.where(own, act, 0.0).astype(BF16)
            act_grad = jnp.where(own, hid_grad * slope, 0.0).astype(BF16)
            out_part += product(hidden, weight_out[e, at, :], 1, 0)
            in_part += product(act_grad, weight_in[e, :, at], 1, 1)
    both[:, :width] = out_part.astype(BF16)
    both[:, width:] = in_part.astype(BF16)


def sum_kernel(count, *refs):
    total = sum(r[...].astype(F32) for r in refs[:count])
    outs = refs[count:]
    rows = outs[0].shape[0]
    for k, out in enumerate(outs):
        out[...] = total[k * rows : (k + 1) * rows].astype(out.dtype)


def sum_of(parts, pieces, dtype):
    rows, columns = parts[0].shape
    return local_call(
        partial(sum_kernel, len(parts)), [((rows // pieces, columns), dtype)] * pieces, *parts
    )


def centre_kernel(count, width, *refs):
    parts = refs[:count]
    slot_sum, stats, out = refs[count:]
    total = sum(r[...].astype(F32) for r in parts).astype(BF16)
    grad_in = total[:, width:].astype(F32)
    centre = jnp.sum(slot_sum[...] * grad_in, axis=1, keepdims=True)
    top, denominator = unpacked(stats[...], 2)
    out[:, : 2 * width] = total
    out[:, 2 * width :] = packed([centre, top, denominator], stats.shape[0]).astype(BF16)


def second_kernel(order, near, far, logits, tokens, out_grad, weights, blocks):
    width = tokens.shape[1]
    half = near.shape[0]

    def against(columns, rows):
        return jnp.concatenate(
            [product(x[:, columns], rows[...], 1, 1) for x in (near, far)], axis=0
        )

    comb_grad = against(slice(0, width), out_grad)
    disp_grad = against(slice(width, 2 * width), tokens)
    stats = jnp.concatenate([x[:, 2 * width :].astype(F32) for x in (near, far)], axis=0)
    centre, top, total = unpacked(stats, 3)
    scores = logits[...]
    dispatch = jnp.exp(scores - top) / total
    combine = softmax_columns(scores)
    comb_mean = jnp.sum(combine * comb_grad, axis=0, keepdims=True)
    logit_grad = dispatch * (disp_grad - centre) + combine * (comb_grad - comb_mean)
    logit_b = logit_grad.astype(BF16)
    weights[: 2 * half] = dispatch.astype(BF16)
    weights[2 * half :] = logit_b
    part = product(logit_b, tokens[...], 1, 0).astype(BF16)
    me = lax.axis_index("exp")
    n_seq, n_exp = lax.axis_size("seq"), lax.axis_size("exp")
    _, rows, share = blocks.shape
    for k, mask in enumerate(order):
        for s in range(n_seq):
            blocks[s * n_exp + (me ^ mask)] = part[
                k * rows : (k + 1) * rows, s * share : (s + 1) * share
            ]


def patch_kernel(weights, near, far, table_near, table_far, out):
    width = out.shape[1]
    rows = jnp.concatenate(
        [x[:, width : 2 * width] for x in (near, far)] + [table_near[...], table_far[...]], axis=0
    )
    out[...] = product(weights[...], rows, 0, 0).astype(BF16)


def shards(tokens, slot_embed, expert_in, expert_out, out_grad):
    width = tokens.shape[1]
    patches = tokens.shape[0]
    own = slot_embed.shape[1]
    n_exp, n_seq = lax.axis_size("exp"), lax.axis_size("seq")
    slots = own * n_exp
    half = slots // 2
    columns = 2 * width + LANES
    chip_groups = groups(n_exp, 2)
    seq_groups = groups(n_seq, 1)

    def gathered_over_chips(x, here):
        for masks in reversed(chip_groups):
            x = here = stack([here] + swaps([x] * len(masks), "exp", masks))
        return x

    table_near = gathered_over_chips(slot_embed.T, loaded(slot_embed.T))
    table_far = swap(table_near, "exp", 1)

    logits, keep, send = local_call(
        first_kernel,
        [((slots, patches), F32), ((half, columns), BF16), ((half, columns), BF16)],
        table_near,
        table_far,
        tokens,
        out_grad,
        limit=12,
    )
    parts = [keep, swap(send, "exp", 1)]
    for masks in chip_groups:
        pieces = merge(parts, width, len(masks) + 1)
        parts = [pieces[0]] + swaps(pieces[1:], "exp", masks)
    for masks in seq_groups:
        (x,) = merge(parts, width, 1)
        parts = [x] + swaps([x] * len(masks), "seq", masks)

    both, slot_sum, stats = local_call(
        partial(expert_kernel, len(parts), width),
        [((own, 2 * width), BF16), ((own, width), F32), ((own, LANES), F32)],
        *parts,
        expert_in,
        expert_out,
        limit=16,
    )
    parts = [both]
    for k, masks in enumerate(seq_groups):
        if k:
            parts = list(sum_of(parts, 1, BF16))
        parts = parts + swaps(parts * len(masks), "seq", masks)
    (packet,) = local_call(
        partial(centre_kernel, len(parts), width),
        [((own, columns), BF16)],
        *parts,
        slot_sum,
        stats,
    )
    near = gathered_over_chips(packet, packet)
    far = swap(near, "exp", 1)

    order = [0]
    for masks in reversed(chip_groups):
        order = [r ^ mask for mask in (0, *masks) for r in order]
    order = order + [r ^ 1 for r in order]
    weights, blocks = local_call(
        partial(second_kernel, order),
        [((2 * slots, patches), BF16), ((n_seq * n_exp, own, width // n_seq), BF16)],
        near,
        far,
        logits,
        tokens,
        out_grad,
        limit=12,
    )
    (tok_grad,) = local_call(
        patch_kernel,
        [((patches, width), BF16)],
        weights,
        near,
        far,
        table_near,
        table_far,
        limit=12,
        to_hbm=(0,),
    )

    part = lax.all_to_all(blocks, ("seq", "exp"), 0, 0, tiled=True)
    part = jnp.sum(part.astype(F32), axis=0)
    return (tok_grad, part.T)


def solution(mesh):
    placed = (
        P(("seq", "exp"), None),
        P(None, "exp"),
        P("exp", None, "seq"),
        P("exp", "seq", None),
        P(("seq", "exp"), None),
    )
    return jax.shard_map(
        shards,
        mesh=mesh,
        in_specs=placed,
        out_specs=(P(("seq", "exp"), None), P("seq", "exp")),
        check_vma=False,
    )
```

```python
from functools import partial
import math

import jax
import jax.numpy as jnp
from jax import lax
from jax.experimental import pallas as pl
from jax.experimental.pallas import tpu as pltpu
from jax.sharding import PartitionSpec as P

LANES = 128
F32 = jnp.float32
BF16 = jnp.bfloat16
MIB = 1 << 20


def swap(x, axis, mask):
    return lax.ppermute(x, axis, [(k, k ^ mask) for k in range(lax.axis_size(axis))])


def swaps(parts, axis, masks):
    return [swap(x, axis, mask) for x, mask in zip(parts, masks)]


def groups(n, first):
    bits = [1 << k for k in range(n.bit_length() - 1) if 1 << k >= first]
    return [
        [b for b in (pair[0], *pair[1:], sum(pair)) if b]
        if len(pair) == 2
        else [pair[0]]
        for pair in (bits[k : k + 2] for k in range(0, len(bits), 2))
    ]


def in_vmem(x):
    return pltpu.with_memory_space_constraint(x, pltpu.VMEM)


def local_call(body, outs, *operands, limit=8, to_hbm=()):
    return pl.pallas_call(
        body,
        out_shape=tuple(
            jax.ShapeDtypeStruct(s, d) if k in to_hbm else pltpu.VMEM(s, d)
            for k, (s, d) in enumerate(outs)
        ),
        in_specs=[pl.BlockSpec(memory_space=pltpu.VMEM)] * len(operands),
        out_specs=tuple(pl.BlockSpec(memory_space=pltpu.VMEM) for _ in outs),
        compiler_params=pltpu.CompilerParams(vmem_limit_bytes=limit * MIB),
        cost_estimate=pl.CostEstimate(flops=10**10, bytes_accessed=4 * MIB, transcendentals=0),
    )(*[in_vmem(x) for x in operands])


def product(left, right, over_left, over_right):
    return lax.dot_general(
        left, right, (((over_left,), (over_right,)), ((), ())), preferred_element_type=F32
    )


def rounded(x):
    return x.astype(BF16).astype(F32)


def packed(columns, rows):
    lane = lax.broadcasted_iota(jnp.int32, (rows, LANES), 1)
    out = jnp.zeros((rows, LANES), F32)
    for k, x in enumerate(columns):
        high = rounded(x)
        mid = rounded(x - high)
        for j, piece in enumerate((high, mid, x - high - mid)):
            out = jnp.where(lane == 3 * k + j, piece, out)
    return out


def unpacked(block, count):
    lane = lax.broadcasted_iota(jnp.int32, block.shape, 1)
    return [
        jnp.sum(
            jnp.where((lane >= 3 * k) & (lane < 3 * k + 3), block, 0.0), axis=1, keepdims=True
        )
        for k in range(count)
    ]


def load_kernel(source, out, semaphore):
    copy = pltpu.make_async_copy(source, out, semaphore)
    copy.start()
    copy.wait()


def loaded(x):
    return pl.pallas_call(
        load_kernel,
        out_shape=pltpu.VMEM(x.shape, x.dtype),
        in_specs=[pl.BlockSpec(memory_space=pl.ANY)],
        out_specs=pl.BlockSpec(memory_space=pltpu.VMEM),
        scratch_shapes=[pltpu.SemaphoreType.DMA],
        compiler_params=pltpu.CompilerParams(vmem_limit_bytes=2 * MIB),
        cost_estimate=pl.CostEstimate(flops=10**9, bytes_accessed=2 * x.size, transcendentals=0),
    )(x)


def concat_kernel(*refs):
    out = refs[-1]
    out[...] = jnp.concatenate([r[...].astype(F32) for r in refs[:-1]], axis=0).astype(BF16)


def stack(parts):
    if len(parts) == 1:
        return parts[0]
    rows = sum(p.shape[0] for p in parts)
    return local_call(concat_kernel, [((rows, parts[0].shape[1]), BF16)], *parts)[0]


def softmax_columns(logits):
    weight = jnp.exp(logits - jnp.max(logits, axis=0, keepdims=True))
    return weight / jnp.sum(weight, axis=0, keepdims=True)


def first_kernel(near, far, tokens, out_grad, logits_out, keep, send):
    width = tokens.shape[1]
    half = near.shape[0]
    logits = jnp.concatenate(
        [product(near[...], tokens[...], 1, 1), product(far[...], tokens[...], 1, 1)], axis=0
    )
    logits_out[...] = logits
    top = jnp.max(logits, axis=1, keepdims=True)
    weight = jnp.exp(logits - top)
    stats = packed([top, jnp.sum(weight, axis=1, keepdims=True)], 2 * half).astype(BF16)
    sums = product(weight.astype(BF16), tokens[...], 1, 0).astype(BF16)
    grads = product(softmax_columns(logits).astype(BF16), out_grad[...], 1, 0).astype(BF16)
    for k, out in enumerate((keep, send)):
        rows = slice(k * half, (k + 1) * half)
        out[:, :width] = sums[rows]
        out[:, width : 2 * width] = grads[rows]
        out[:, 2 * width :] = stats[rows]


def merged(refs, width):
    stats = [unpacked(r[:, 2 * width :].astype(F32), 2) for r in refs]
    top = stats[0][0]
    for other, _ in stats[1:]:
        top = jnp.maximum(top, other)
    scales = [jnp.exp(t - top) for t, _ in stats]
    total = sum(s * l for s, (_, l) in zip(scales, stats))
    sums = sum(s * r[:, :width].astype(F32) for s, r in zip(scales, refs))
    grads = sum(r[:, width : 2 * width].astype(F32) for r in refs)
    return sums, grads, top, total


def merge_kernel(count, width, *refs):
    sums, grads, top, total = merged(refs[:count], width)
    outs = refs[count:]
    rows = outs[0].shape[0]
    stats = packed([top, total], sums.shape[0])
    places = [0, *reversed(range(1, len(outs)))]
    for k, out in zip(places, outs):
        part = slice(k * rows, (k + 1) * rows)
        out[:, :width] = sums[part].astype(BF16)
        out[:, width : 2 * width] = grads[part].astype(BF16)
        out[:, 2 * width :] = stats[part].astype(BF16)


def merge(parts, width, pieces):
    rows, columns = parts[0].shape
    return local_call(
        partial(merge_kernel, len(parts), width),
        [((rows // pieces, columns), BF16)] * pieces,
        *parts,
    )


def gelu_and_slope(v):
    root = math.sqrt(2.0 / math.pi)
    t = jnp.tanh(root * (v + 0.044715 * (v * v * v)))
    slope = 0.5 * (1.0 + t) + 0.5 * v * (1.0 - t * t) * (root * (1.0 + 3 * 0.044715 * (v * v)))
    return 0.5 * v * (1.0 + t), slope


def expert_kernel(count, width, *refs):
    parts = refs[:count]
    weight_in, weight_out, both, slot_sum, stats = refs[count:]
    sums, grads, top, total = merged(parts, width)
    stats[...] = packed([top, total], stats.shape[0])
    sums = sums / total
    slot_sum[...] = sums
    slot_in, grad_out = sums.astype(BF16), grads.astype(BF16)
    experts, _, units = weight_in.shape
    rows = sums.shape[0]
    step = min(units, 512)
    row = lax.broadcasted_iota(jnp.int32, (rows, step), 0)
    out_part = jnp.zeros((rows, width), F32)
    in_part = jnp.zeros((rows, width), F32)
    for e in range(experts):
        own = (row >= e * (rows // experts)) & (row < (e + 1) * (rows // experts))
        for c in range(units // step):
            at = slice(c * step, (c + 1) * step)
            pre_act = product(slot_in, weight_in[e, :, at], 1, 0)
            hid_grad = product(grad_out, weight_out[e, at, :], 1, 1)
            act, slope = gelu_and_slope(pre_act)
            hidden = jnp.where(own, act, 0.0).astype(BF16)
            act_grad = jnp.where(own, hid_grad * slope, 0.0).astype(BF16)
            out_part += product(hidden, weight_out[e, at, :], 1, 0)
            in_part += product(act_grad, weight_in[e, :, at], 1, 1)
    both[:, :width] = out_part.astype(BF16)
    both[:, width:] = in_part.astype(BF16)


def sum_kernel(count, *refs):
    total = sum(r[...].astype(F32) for r in refs[:count])
    outs = refs[count:]
    rows = outs[0].shape[0]
    for k, out in enumerate(outs):
        out[...] = total[k * rows : (k + 1) * rows].astype(out.dtype)


def sum_of(parts, pieces, dtype):
    rows, columns = parts[0].shape
    return local_call(
        partial(sum_kernel, len(parts)), [((rows // pieces, columns), dtype)] * pieces, *parts
    )


def centre_kernel(count, width, *refs):
    parts = refs[:count]
    slot_sum, stats, out = refs[count:]
    total = sum(r[...].astype(F32) for r in parts).astype(BF16)
    grad_in = total[:, width:].astype(F32)
    centre = jnp.sum(slot_sum[...] * grad_in, axis=1, keepdims=True)
    top, denominator = unpacked(stats[...], 2)
    out[:, : 2 * width] = total
    out[:, 2 * width :] = packed([centre, top, denominator], stats.shape[0]).astype(BF16)


def second_kernel(order, near, far, logits, tokens, out_grad, weights, blocks):
    width = tokens.shape[1]
    half = near.shape[0]

    def against(columns, rows):
        return jnp.concatenate(
            [product(x[:, columns], rows[...], 1, 1) for x in (near, far)], axis=0
        )

    comb_grad = against(slice(0, width), out_grad)
    disp_grad = against(slice(width, 2 * width), tokens)
    stats = jnp.concatenate([x[:, 2 * width :].astype(F32) for x in (near, far)], axis=0)
    centre, top, total = unpacked(stats, 3)
    scores = logits[...]
    dispatch = jnp.exp(scores - top) / total
    combine = softmax_columns(scores)
    comb_mean = jnp.sum(combine * comb_grad, axis=0, keepdims=True)
    logit_grad = dispatch * (disp_grad - centre) + combine * (comb_grad - comb_mean)
    logit_b = logit_grad.astype(BF16)
    weights[: 2 * half] = dispatch.astype(BF16)
    weights[2 * half :] = logit_b
    part = product(logit_b, tokens[...], 1, 0).astype(BF16)
    me = lax.axis_index("exp")
    n_seq, n_exp = lax.axis_size("seq"), lax.axis_size("exp")
    _, rows, share = blocks.shape
    for k, mask in enumerate(order):
        for s in range(n_seq):
            blocks[s * n_exp + (me ^ mask)] = part[
                k * rows : (k + 1) * rows, s * share : (s + 1) * share
            ]


def patch_kernel(weights, near, far, table_near, table_far, out):
    width = out.shape[1]
    rows = jnp.concatenate(
        [x[:, width : 2 * width] for x in (near, far)] + [table_near[...], table_far[...]], axis=0
    )
    out[...] = product(weights[...], rows, 0, 0).astype(BF16)


def shards(tokens, slot_embed, expert_in, expert_out, out_grad):
    width = tokens.shape[1]
    patches = tokens.shape[0]
    own = slot_embed.shape[1]
    n_exp, n_seq = lax.axis_size("exp"), lax.axis_size("seq")
    slots = own * n_exp
    half = slots // 2
    columns = 2 * width + LANES
    chip_groups = groups(n_exp, 2)
    seq_groups = groups(n_seq, 1)

    def gathered_over_chips(x, here):
        for masks in reversed(chip_groups):
            x = here = stack([here] + swaps([x] * len(masks), "exp", masks))
        return x

    table_near = gathered_over_chips(slot_embed.T, loaded(slot_embed.T))
    table_far = swap(table_near, "exp", 1)

    logits, keep, send = local_call(
        first_kernel,
        [((slots, patches), F32), ((half, columns), BF16), ((half, columns), BF16)],
        table_near,
        table_far,
        tokens,
        out_grad,
        limit=12,
    )
    parts = [keep, swap(send, "exp", 1)]
    for masks in chip_groups:
        pieces = merge(parts, width, len(masks) + 1)
        parts = [pieces[0]] + swaps(pieces[1:], "exp", masks[::-1])
    for masks in seq_groups:
        (x,) = merge(parts, width, 1)
        parts = [x] + swaps([x] * len(masks), "seq", masks)

    both, slot_sum, stats = local_call(
        partial(expert_kernel, len(parts), width),
        [((own, 2 * width), BF16), ((own, width), F32), ((own, LANES), F32)],
        *parts,
        expert_in,
        expert_out,
        limit=16,
    )
    parts = [both]
    for k, masks in enumerate(seq_groups):
        if k:
            parts = list(sum_of(parts, 1, BF16))
        parts = parts + swaps(parts * len(masks), "seq", masks)
    (packet,) = local_call(
        partial(centre_kernel, len(parts), width),
        [((own, columns), BF16)],
        *parts,
        slot_sum,
        stats,
    )
    near = gathered_over_chips(packet, packet)
    far = swap(near, "exp", 1)

    order = [0]
    for masks in reversed(chip_groups):
        order = [r ^ mask for mask in (0, *masks) for r in order]
    order = order + [r ^ 1 for r in order]
    weights, blocks = local_call(
        partial(second_kernel, order),
        [((2 * slots, patches), BF16), ((n_seq * n_exp, own, width // n_seq), BF16)],
        near,
        far,
        logits,
        tokens,
        out_grad,
        limit=12,
    )
    (tok_grad,) = local_call(
        patch_kernel,
        [((patches, width), BF16)],
        weights,
        near,
        far,
        table_near,
        table_far,
        limit=12,
        to_hbm=(0,),
    )

    part = lax.all_to_all(blocks, ("seq", "exp"), 0, 0, tiled=True)
    part = jnp.sum(part.astype(F32), axis=0)
    return (tok_grad, part.T)


def solution(mesh):
    placed = (
        P(("seq", "exp"), None),
        P(None, "exp"),
        P("exp", None, "seq"),
        P("exp", "seq", None),
        P(("seq", "exp"), None),
    )
    return jax.shard_map(
        shards,
        mesh=mesh,
        in_specs=placed,
        out_specs=(P(("seq", "exp"), None), P("seq", "exp")),
        check_vma=False,
    )
```

```python
from functools import partial
import math

import jax
import jax.numpy as jnp
from jax import lax
from jax.experimental import pallas as pl
from jax.experimental.pallas import tpu as pltpu
from jax.sharding import PartitionSpec as P

LANES = 128
F32 = jnp.float32
BF16 = jnp.bfloat16
MIB = 1 << 20


def swap(x, axis, mask):
    return lax.ppermute(x, axis, [(k, k ^ mask) for k in range(lax.axis_size(axis))])


def swaps(parts, axis, masks):
    return [swap(x, axis, mask) for x, mask in zip(parts, masks)]


def groups(n, first):
    bits = [1 << k for k in range(n.bit_length() - 1) if 1 << k >= first]
    return [
        [b for b in (pair[0], *pair[1:], sum(pair)) if b]
        if len(pair) == 2
        else [pair[0]]
        for pair in (bits[k : k + 2] for k in range(0, len(bits), 2))
    ]


def in_vmem(x):
    return pltpu.with_memory_space_constraint(x, pltpu.VMEM)


def local_call(body, outs, *operands, limit=8, to_hbm=(), loose=(), flops=10**10):
    return pl.pallas_call(
        body,
        out_shape=tuple(
            jax.ShapeDtypeStruct(s, d) if k in to_hbm else pltpu.VMEM(s, d)
            for k, (s, d) in enumerate(outs)
        ),
        in_specs=[pl.BlockSpec(memory_space=pltpu.VMEM)] * len(operands),
        out_specs=tuple(pl.BlockSpec(memory_space=pltpu.VMEM) for _ in outs),
        compiler_params=pltpu.CompilerParams(vmem_limit_bytes=limit * MIB),
        cost_estimate=pl.CostEstimate(flops=flops, bytes_accessed=4 * MIB, transcendentals=0),
    )(*[in_vmem(x) for x in operands])


def product(left, right, over_left, over_right):
    return lax.dot_general(
        left, right, (((over_left,), (over_right,)), ((), ())), preferred_element_type=F32
    )


def rounded(x):
    return x.astype(BF16).astype(F32)


def packed(columns, rows):
    lane = lax.broadcasted_iota(jnp.int32, (rows, LANES), 1)
    out = jnp.zeros((rows, LANES), F32)
    for k, x in enumerate(columns):
        high = rounded(x)
        mid = rounded(x - high)
        for j, piece in enumerate((high, mid, x - high - mid)):
            out = jnp.where(lane == 3 * k + j, piece, out)
    return out


def unpacked(block, count):
    lane = lax.broadcasted_iota(jnp.int32, block.shape, 1)
    return [
        jnp.sum(
            jnp.where((lane >= 3 * k) & (lane < 3 * k + 3), block, 0.0), axis=1, keepdims=True
        )
        for k in range(count)
    ]


def load_kernel(source, out, semaphore):
    copy = pltpu.make_async_copy(source, out, semaphore)
    copy.start()
    copy.wait()


def loaded(x):
    return pl.pallas_call(
        load_kernel,
        out_shape=pltpu.VMEM(x.shape, x.dtype),
        in_specs=[pl.BlockSpec(memory_space=pl.ANY)],
        out_specs=pl.BlockSpec(memory_space=pltpu.VMEM),
        scratch_shapes=[pltpu.SemaphoreType.DMA],
        compiler_params=pltpu.CompilerParams(vmem_limit_bytes=2 * MIB),
        cost_estimate=pl.CostEstimate(flops=10**9, bytes_accessed=2 * x.size, transcendentals=0),
    )(x)


def concat_kernel(*refs):
    out = refs[-1]
    out[...] = jnp.concatenate([r[...].astype(F32) for r in refs[:-1]], axis=0).astype(BF16)


def stack(parts):
    if len(parts) == 1:
        return parts[0]
    rows = sum(p.shape[0] for p in parts)
    return local_call(concat_kernel, [((rows, parts[0].shape[1]), BF16)], *parts)[0]


def softmax_columns(logits):
    weight = jnp.exp(logits - jnp.max(logits, axis=0, keepdims=True))
    return weight / jnp.sum(weight, axis=0, keepdims=True)


def first_kernel(near, far, tokens, out_grad, logits_out, keep, send):
    width = tokens.shape[1]
    half = near.shape[0]
    logits = jnp.concatenate(
        [product(near[...], tokens[...], 1, 1), product(far[...], tokens[...], 1, 1)], axis=0
    )
    logits_out[...] = logits
    top = jnp.max(logits, axis=1, keepdims=True)
    weight = jnp.exp(logits - top)
    stats = packed([top, jnp.sum(weight, axis=1, keepdims=True)], 2 * half).astype(BF16)
    sums = product(weight.astype(BF16), tokens[...], 1, 0).astype(BF16)
    grads = product(softmax_columns(logits).astype(BF16), out_grad[...], 1, 0).astype(BF16)
    for k, out in enumerate((keep, send)):
        rows = slice(k * half, (k + 1) * half)
        out[:, :width] = sums[rows]
        out[:, width : 2 * width] = grads[rows]
        out[:, 2 * width :] = stats[rows]


def merged(refs, width):
    stats = [unpacked(r[:, 2 * width :].astype(F32), 2) for r in refs]
    top = stats[0][0]
    for other, _ in stats[1:]:
        top = jnp.maximum(top, other)
    scales = [jnp.exp(t - top) for t, _ in stats]
    total = sum(s * l for s, (_, l) in zip(scales, stats))
    sums = sum(s * r[:, :width].astype(F32) for s, r in zip(scales, refs))
    grads = sum(r[:, width : 2 * width].astype(F32) for r in refs)
    return sums, grads, top, total


def merge_kernel(count, width, *refs):
    sums, grads, top, total = merged(refs[:count], width)
    outs = refs[count:]
    rows = outs[0].shape[0]
    stats = packed([top, total], sums.shape[0])
    places = [0, *reversed(range(1, len(outs)))]
    for k, out in zip(places, outs):
        part = slice(k * rows, (k + 1) * rows)
        out[:, :width] = sums[part].astype(BF16)
        out[:, width : 2 * width] = grads[part].astype(BF16)
        out[:, 2 * width :] = stats[part].astype(BF16)


def merge(parts, width, pieces):
    rows, columns = parts[0].shape
    return local_call(
        partial(merge_kernel, len(parts), width),
        [((rows // pieces, columns), BF16)] * pieces,
        *parts,
    )


def flip_kernel(index, weight, after, out):
    out[...] = weight[index].T


def flipped(weights, after):
    experts, rows, columns = weights.shape
    return [
        local_call(
            partial(flip_kernel, e), [((columns, rows), BF16)], weights, after, flops=10**9
        )[0]
        for e in range(experts)
    ]


def gelu_and_slope(v):
    root = math.sqrt(2.0 / math.pi)
    t = jnp.tanh(root * (v + 0.044715 * (v * v * v)))
    slope = 0.5 * (1.0 + t) + 0.5 * v * (1.0 - t * t) * (root * (1.0 + 3 * 0.044715 * (v * v)))
    return 0.5 * v * (1.0 + t), slope


def expert_kernel(count, width, *refs):
    parts = refs[:count]
    weight_in, weight_out = refs[count : count + 2]
    experts, _, units = weight_in.shape
    flips = refs[count + 2 : count + 2 + 2 * experts]
    in_flipped, out_flipped = flips[:experts], flips[experts:]
    both, slot_sum, stats = refs[count + 2 + 2 * experts :]
    sums, grads, top, total = merged(parts, width)
    stats[...] = packed([top, total], stats.shape[0])
    sums = sums / total
    slot_sum[...] = sums
    slot_in, grad_out = sums.astype(BF16), grads.astype(BF16)
    rows = sums.shape[0]
    step = min(units, 512)
    row = lax.broadcasted_iota(jnp.int32, (rows, step), 0)
    out_part = jnp.zeros((rows, width), F32)
    in_part = jnp.zeros((rows, width), F32)
    for e in range(experts):
        own = (row >= e * (rows // experts)) & (row < (e + 1) * (rows // experts))
        for c in range(units // step):
            at = slice(c * step, (c + 1) * step)
            pre_act = product(slot_in, weight_in[e, :, at], 1, 0)
            hid_grad = product(grad_out, out_flipped[e][:, at], 1, 0)
            act, slope = gelu_and_slope(pre_act)
            hidden = jnp.where(own, act, 0.0).astype(BF16)
            act_grad = jnp.where(own, hid_grad * slope, 0.0).astype(BF16)
            out_part += product(hidden, weight_out[e, at, :], 1, 0)
            in_part += product(act_grad, in_flipped[e][at, :], 1, 0)
    both[:, :width] = out_part.astype(BF16)
    both[:, width:] = in_part.astype(BF16)


def sum_kernel(count, *refs):
    total = sum(r[...].astype(F32) for r in refs[:count])
    outs = refs[count:]
    rows = outs[0].shape[0]
    for k, out in enumerate(outs):
        out[...] = total[k * rows : (k + 1) * rows].astype(out.dtype)


def sum_of(parts, pieces, dtype):
    rows, columns = parts[0].shape
    return local_call(
        partial(sum_kernel, len(parts)), [((rows // pieces, columns), dtype)] * pieces, *parts
    )


def centre_kernel(count, width, *refs):
    parts = refs[:count]
    slot_sum, stats, out = refs[count:]
    total = sum(r[...].astype(F32) for r in parts).astype(BF16)
    grad_in = total[:, width:].astype(F32)
    centre = jnp.sum(slot_sum[...] * grad_in, axis=1, keepdims=True)
    top, denominator = unpacked(stats[...], 2)
    out[:, : 2 * width] = total
    out[:, 2 * width :] = packed([centre, top, denominator], stats.shape[0]).astype(BF16)


def second_kernel(order, near, far, logits, tokens, out_grad, weights, blocks):
    width = tokens.shape[1]
    half = near.shape[0]

    def against(columns, rows):
        return jnp.concatenate(
            [product(x[:, columns], rows[...], 1, 1) for x in (near, far)], axis=0
        )

    comb_grad = against(slice(0, width), out_grad)
    disp_grad = against(slice(width, 2 * width), tokens)
    stats = jnp.concatenate([x[:, 2 * width :].astype(F32) for x in (near, far)], axis=0)
    centre, top, total = unpacked(stats, 3)
    scores = logits[...]
    dispatch = jnp.exp(scores - top) / total
    combine = softmax_columns(scores)
    comb_mean = jnp.sum(combine * comb_grad, axis=0, keepdims=True)
    logit_grad = dispatch * (disp_grad - centre) + combine * (comb_grad - comb_mean)
    logit_b = logit_grad.astype(BF16)
    weights[: 2 * half] = dispatch.astype(BF16)
    weights[2 * half :] = logit_b
    part = product(logit_b, tokens[...], 1, 0).astype(BF16)
    me = lax.axis_index("exp")
    n_seq, n_exp = lax.axis_size("seq"), lax.axis_size("exp")
    _, rows, share = blocks.shape
    for k, mask in enumerate(order):
        for s in range(n_seq):
            blocks[s * n_exp + (me ^ mask)] = part[
                k * rows : (k + 1) * rows, s * share : (s + 1) * share
            ]


def patch_kernel(weights, near, far, table_near, table_far, out):
    width = out.shape[1]
    rows = jnp.concatenate(
        [x[:, width : 2 * width] for x in (near, far)] + [table_near[...], table_far[...]], axis=0
    )
    out[...] = product(weights[...], rows, 0, 0).astype(BF16)


def shards(tokens, slot_embed, expert_in, expert_out, out_grad):
    width = tokens.shape[1]
    patches = tokens.shape[0]
    own = slot_embed.shape[1]
    n_exp, n_seq = lax.axis_size("exp"), lax.axis_size("seq")
    slots = own * n_exp
    half = slots // 2
    columns = 2 * width + LANES
    chip_groups = groups(n_exp, 2)
    seq_groups = groups(n_seq, 1)

    def gathered_over_chips(x, here):
        for masks in reversed(chip_groups):
            x = here = stack([here] + swaps([x] * len(masks), "exp", masks))
        return x

    table_near = gathered_over_chips(slot_embed.T, loaded(slot_embed.T))
    table_far = swap(table_near, "exp", 1)

    logits, keep, send = local_call(
        first_kernel,
        [((slots, patches), F32), ((half, columns), BF16), ((half, columns), BF16)],
        table_near,
        table_far,
        tokens,
        out_grad,
        limit=12,
    )
    parts = [keep, swap(send, "exp", 1)]
    for masks in chip_groups:
        pieces = merge(parts, width, len(masks) + 1)
        parts = [pieces[0]] + swaps(pieces[1:], "exp", masks[::-1])
    own_piece = pieces[0]
    for masks in seq_groups:
        (x,) = merge(parts, width, 1)
        parts = [x] + swaps([x] * len(masks), "seq", masks)
    own_sum = x

    both, slot_sum, stats = local_call(
        partial(expert_kernel, len(parts), width),
        [((own, 2 * width), BF16), ((own, width), F32), ((own, LANES), F32)],
        *parts,
        expert_in,
        expert_out,
        *flipped(expert_in, own_sum),
        *flipped(expert_out, own_piece),
        limit=16,
    )
    parts = [both]
    for k, masks in enumerate(seq_groups):
        if k:
            parts = list(sum_of(parts, 1, BF16))
        parts = parts + swaps(parts * len(masks), "seq", masks)
    (packet,) = local_call(
        partial(centre_kernel, len(parts), width),
        [((own, columns), BF16)],
        *parts,
        slot_sum,
        stats,
    )
    near = gathered_over_chips(packet, packet)
    far = swap(near, "exp", 1)

    order = [0]
    for masks in reversed(chip_groups):
        order = [r ^ mask for mask in (0, *masks) for r in order]
    order = order + [r ^ 1 for r in order]
    weights, blocks = local_call(
        partial(second_kernel, order),
        [((2 * slots, patches), BF16), ((n_seq * n_exp, own, width // n_seq), BF16)],
        near,
        far,
        logits,
        tokens,
        out_grad,
        limit=12,
    )
    (tok_grad,) = local_call(
        patch_kernel,
        [((patches, width), BF16)],
        weights,
        near,
        far,
        table_near,
        table_far,
        limit=12,
        to_hbm=(0,),
    )

    part = lax.all_to_all(blocks, ("seq", "exp"), 0, 0, tiled=True)
    part = jnp.sum(part.astype(F32), axis=0)
    return (tok_grad, part.T)


def solution(mesh):
    placed = (
        P(("seq", "exp"), None),
        P(None, "exp"),
        P("exp", None, "seq"),
        P("exp", "seq", None),
        P(("seq", "exp"), None),
    )
    return jax.shard_map(
        shards,
        mesh=mesh,
        in_specs=placed,
        out_specs=(P(("seq", "exp"), None), P("seq", "exp")),
        check_vma=False,
    )
```

```python
from functools import partial
import math

import jax
import jax.numpy as jnp
from jax import lax
from jax.experimental import pallas as pl
from jax.experimental.pallas import tpu as pltpu
from jax.sharding import PartitionSpec as P

LANES = 128
F32 = jnp.float32
BF16 = jnp.bfloat16
MIB = 1 << 20


def swap(x, axis, mask):
    return lax.ppermute(x, axis, [(k, k ^ mask) for k in range(lax.axis_size(axis))])


def swaps(parts, axis, masks):
    return [swap(x, axis, mask) for x, mask in zip(parts, masks)]


def to_all(x, axis, masks):
    return swaps([x] * len(masks), axis, masks)


def groups(n, first):
    bits = [1 << k for k in range(n.bit_length() - 1) if 1 << k >= first]
    return [
        [sum(pair), pair[1], pair[0]]
        if len(pair) == 2
        else [pair[0]]
        for pair in (bits[k : k + 2] for k in range(0, len(bits), 2))
    ]


def in_vmem(x):
    return pltpu.with_memory_space_constraint(x, pltpu.VMEM)


def local_call(body, outs, *operands, limit=8, to_hbm=(), loose=(), flops=10**10):
    return pl.pallas_call(
        body,
        out_shape=tuple(
            jax.ShapeDtypeStruct(s, d) if k in to_hbm else pltpu.VMEM(s, d)
            for k, (s, d) in enumerate(outs)
        ),
        in_specs=[pl.BlockSpec(memory_space=pltpu.VMEM)] * len(operands),
        out_specs=tuple(pl.BlockSpec(memory_space=pltpu.VMEM) for _ in outs),
        compiler_params=pltpu.CompilerParams(vmem_limit_bytes=limit * MIB),
        cost_estimate=pl.CostEstimate(flops=flops, bytes_accessed=4 * MIB, transcendentals=0),
    )(*[in_vmem(x) for x in operands])


def product(left, right, over_left, over_right):
    return lax.dot_general(
        left, right, (((over_left,), (over_right,)), ((), ())), preferred_element_type=F32
    )


def rounded(x):
    return x.astype(BF16).astype(F32)


def packed(columns, rows):
    lane = lax.broadcasted_iota(jnp.int32, (rows, LANES), 1)
    out = jnp.zeros((rows, LANES), F32)
    for k, x in enumerate(columns):
        high = rounded(x)
        mid = rounded(x - high)
        for j, piece in enumerate((high, mid, x - high - mid)):
            out = jnp.where(lane == 3 * k + j, piece, out)
    return out


def unpacked(block, count):
    lane = lax.broadcasted_iota(jnp.int32, block.shape, 1)
    return [
        jnp.sum(
            jnp.where((lane >= 3 * k) & (lane < 3 * k + 3), block, 0.0), axis=1, keepdims=True
        )
        for k in range(count)
    ]


def load_kernel(source, out, semaphore):
    copy = pltpu.make_async_copy(source, out, semaphore)
    copy.start()
    copy.wait()


def loaded(x):
    return pl.pallas_call(
        load_kernel,
        out_shape=pltpu.VMEM(x.shape, x.dtype),
        in_specs=[pl.BlockSpec(memory_space=pl.ANY)],
        out_specs=pl.BlockSpec(memory_space=pltpu.VMEM),
        scratch_shapes=[pltpu.SemaphoreType.DMA],
        compiler_params=pltpu.CompilerParams(vmem_limit_bytes=2 * MIB),
        cost_estimate=pl.CostEstimate(flops=10**9, bytes_accessed=2 * x.size, transcendentals=0),
    )(x)


def concat_kernel(*refs):
    out = refs[-1]
    out[...] = jnp.concatenate([r[...].astype(F32) for r in refs[:-1]], axis=0).astype(BF16)


def stack(parts):
    if len(parts) == 1:
        return parts[0]
    rows = sum(p.shape[0] for p in parts)
    return local_call(concat_kernel, [((rows, parts[0].shape[1]), BF16)], *parts)[0]


def softmax_columns(logits):
    weight = jnp.exp(logits - jnp.max(logits, axis=0, keepdims=True))
    return weight / jnp.sum(weight, axis=0, keepdims=True)


def first_kernel(near, far, tokens_flipped, tokens, out_grad, logits_out, keep, send):
    width = tokens.shape[1]
    half = near.shape[0]
    logits = jnp.concatenate(
        [product(x[...], tokens_flipped[...], 1, 0) for x in (near, far)], axis=0
    )
    logits_out[...] = logits
    top = jnp.max(logits, axis=1, keepdims=True)
    weight = jnp.exp(logits - top)
    stats = packed([top, jnp.sum(weight, axis=1, keepdims=True)], 2 * half).astype(BF16)
    sums = product(weight.astype(BF16), tokens[...], 1, 0).astype(BF16)
    grads = product(softmax_columns(logits).astype(BF16), out_grad[...], 1, 0).astype(BF16)
    for k, out in enumerate((keep, send)):
        rows = slice(k * half, (k + 1) * half)
        out[:, :width] = sums[rows]
        out[:, width : 2 * width] = grads[rows]
        out[:, 2 * width :] = stats[rows]


def merged(refs, width):
    stats = [unpacked(r[:, 2 * width :].astype(F32), 2) for r in refs]
    top = stats[0][0]
    for other, _ in stats[1:]:
        top = jnp.maximum(top, other)
    scales = [jnp.exp(t - top) for t, _ in stats]
    total = sum(s * l for s, (_, l) in zip(scales, stats))
    sums = sum(s * r[:, :width].astype(F32) for s, r in zip(scales, refs))
    grads = sum(r[:, width : 2 * width].astype(F32) for r in refs)
    return sums, grads, top, total


def merge_kernel(count, width, *refs):
    sums, grads, top, total = merged(refs[:count], width)
    outs = refs[count:]
    rows = outs[0].shape[0]
    stats = packed([top, total], sums.shape[0])
    for k, out in enumerate(outs):
        part = slice(k * rows, (k + 1) * rows)
        out[:, :width] = sums[part].astype(BF16)
        out[:, width : 2 * width] = grads[part].astype(BF16)
        out[:, 2 * width :] = stats[part].astype(BF16)


def merge(parts, width, pieces):
    rows, columns = parts[0].shape
    return local_call(
        partial(merge_kernel, len(parts), width),
        [((rows // pieces, columns), BF16)] * pieces,
        *parts,
    )


def flip_kernel(index, weight, after, out):
    out[...] = weight[index].T


def flip_whole_kernel(x, out):
    out[...] = x[...].T


def flipped_whole(x):
    shape = (x.shape[1], x.shape[0])
    return local_call(flip_whole_kernel, [(shape, BF16)], x, flops=3 * 10**8)[0]


def flipped(weights, after):
    experts, rows, columns = weights.shape
    return [
        local_call(
            partial(flip_kernel, e), [((columns, rows), BF16)], weights, after, flops=10**9
        )[0]
        for e in range(experts)
    ]


def gelu_and_slope(v):
    root = math.sqrt(2.0 / math.pi)
    t = jnp.tanh(root * (v + 0.044715 * (v * v * v)))
    slope = 0.5 * (1.0 + t) + 0.5 * v * (1.0 - t * t) * (root * (1.0 + 3 * 0.044715 * (v * v)))
    return 0.5 * v * (1.0 + t), slope


def expert_kernel(count, width, *refs):
    parts = refs[:count]
    weight_in, weight_out = refs[count : count + 2]
    experts, _, units = weight_in.shape
    flips = refs[count + 2 : count + 2 + 2 * experts]
    in_flipped, out_flipped = flips[:experts], flips[experts:]
    both, slot_sum, stats = refs[count + 2 + 2 * experts :]
    sums, grads, top, total = merged(parts, width)
    stats[...] = packed([top, total], stats.shape[0])
    sums = sums / total
    slot_sum[...] = sums
    slot_in, grad_out = sums.astype(BF16), grads.astype(BF16)
    rows = sums.shape[0]
    step = min(units, 512)
    row = lax.broadcasted_iota(jnp.int32, (rows, step), 0)
    out_part = jnp.zeros((rows, width), F32)
    in_part = jnp.zeros((rows, width), F32)
    for e in range(experts):
        own = (row >= e * (rows // experts)) & (row < (e + 1) * (rows // experts))
        for c in range(units // step):
            at = slice(c * step, (c + 1) * step)
            pre_act = product(slot_in, weight_in[e, :, at], 1, 0)
            hid_grad = product(grad_out, out_flipped[e][:, at], 1, 0)
            act, slope = gelu_and_slope(pre_act)
            hidden = jnp.where(own, act, 0.0).astype(BF16)
            act_grad = jnp.where(own, hid_grad * slope, 0.0).astype(BF16)
            out_part += product(hidden, weight_out[e, at, :], 1, 0)
            in_part += product(act_grad, in_flipped[e][at, :], 1, 0)
    both[:, :width] = out_part.astype(BF16)
    both[:, width:] = in_part.astype(BF16)


def sum_kernel(count, *refs):
    total = sum(r[...].astype(F32) for r in refs[:count])
    outs = refs[count:]
    rows = outs[0].shape[0]
    for k, out in enumerate(outs):
        out[...] = total[k * rows : (k + 1) * rows].astype(out.dtype)


def sum_of(parts, pieces, dtype):
    rows, columns = parts[0].shape
    return local_call(
        partial(sum_kernel, len(parts)), [((rows // pieces, columns), dtype)] * pieces, *parts
    )


def centre_kernel(count, width, *refs):
    parts = refs[:count]
    slot_sum, stats, out = refs[count:]
    total = sum(r[...].astype(F32) for r in parts).astype(BF16)
    grad_in = total[:, width:].astype(F32)
    centre = jnp.sum(slot_sum[...] * grad_in, axis=1, keepdims=True)
    top, denominator = unpacked(stats[...], 2)
    out[:, : 2 * width] = total
    out[:, 2 * width :] = packed([centre, top, denominator], stats.shape[0]).astype(BF16)


def second_kernel(
    order, near, far, logits, tokens_flipped, tokens, out_grad_flipped, weights, blocks
):
    width = tokens.shape[1]
    half = near.shape[0]

    def against(columns, rows):
        both = jnp.concatenate([near[:, columns], far[:, columns]], axis=0)
        return product(both, rows[...], 1, 0)

    comb_grad = against(slice(0, width), out_grad_flipped)
    disp_grad = against(slice(width, 2 * width), tokens_flipped)
    stats = jnp.concatenate([x[:, 2 * width :].astype(F32) for x in (near, far)], axis=0)
    centre, top, total = unpacked(stats, 3)
    scores = logits[...]
    dispatch = jnp.exp(scores - top) / total
    combine = softmax_columns(scores)
    comb_mean = jnp.sum(combine * comb_grad, axis=0, keepdims=True)
    logit_grad = dispatch * (disp_grad - centre) + combine * (comb_grad - comb_mean)
    logit_b = logit_grad.astype(BF16)
    weights[: 2 * half] = dispatch.astype(BF16)
    weights[2 * half :] = logit_b
    part = product(logit_b, tokens[...], 1, 0).astype(BF16)
    me = lax.axis_index("exp")
    n_seq, n_exp = lax.axis_size("seq"), lax.axis_size("exp")
    _, rows, share = blocks.shape
    for k, mask in enumerate(order):
        for s in range(n_seq):
            blocks[s * n_exp + (me ^ mask)] = part[
                k * rows : (k + 1) * rows, s * share : (s + 1) * share
            ]


def patch_kernel(weights, near, far, table_near, table_far, out):
    width = out.shape[1]
    rows = jnp.concatenate(
        [x[:, width : 2 * width] for x in (near, far)] + [table_near[...], table_far[...]], axis=0
    )
    out[...] = product(weights[...], rows, 0, 0).astype(BF16)


def shards(tokens, slot_embed, expert_in, expert_out, out_grad):
    width = tokens.shape[1]
    patches = tokens.shape[0]
    own = slot_embed.shape[1]
    n_exp, n_seq = lax.axis_size("exp"), lax.axis_size("seq")
    slots = own * n_exp
    half = slots // 2
    columns = 2 * width + LANES
    chip_groups = groups(n_exp, 2)
    seq_groups = groups(n_seq, 1)

    def gathered_over_chips(x, here):
        for masks in reversed(chip_groups):
            x = here = stack([here] + to_all(x, "exp", masks))
        return x

    table_near = gathered_over_chips(slot_embed.T, loaded(slot_embed.T))
    table_far = swap(table_near, "exp", 1)

    tokens_flipped, out_grad_flipped = flipped_whole(tokens), flipped_whole(out_grad)
    logits, keep, send = local_call(
        first_kernel,
        [((slots, patches), F32), ((half, columns), BF16), ((half, columns), BF16)],
        table_near,
        table_far,
        tokens_flipped,
        tokens,
        out_grad,
        limit=12,
    )
    parts = [keep, swap(send, "exp", 1)]
    for masks in chip_groups:
        pieces = merge(parts, width, len(masks) + 1)
        parts = [pieces[0]] + swaps(pieces[1:], "exp", masks)
    own_piece = pieces[0]
    for masks in seq_groups:
        (x,) = merge(parts, width, 1)
        parts = [x] + to_all(x, "seq", masks)
    own_sum = x

    both, slot_sum, stats = local_call(
        partial(expert_kernel, len(parts), width),
        [((own, 2 * width), BF16), ((own, width), F32), ((own, LANES), F32)],
        *parts,
        expert_in,
        expert_out,
        *flipped(expert_in, own_sum),
        *flipped(expert_out, own_piece),
        limit=16,
    )
    parts = [both]
    for k, masks in enumerate(seq_groups):
        if k:
            parts = list(sum_of(parts, 1, BF16))
        parts = parts + to_all(parts[0], "seq", masks)
    (packet,) = local_call(
        partial(centre_kernel, len(parts), width),
        [((own, columns), BF16)],
        *parts,
        slot_sum,
        stats,
    )
    near = gathered_over_chips(packet, packet)
    far = swap(near, "exp", 1)

    order = [0]
    for masks in reversed(chip_groups):
        order = [r ^ mask for mask in (0, *masks) for r in order]
    order = order + [r ^ 1 for r in order]
    weights, blocks = local_call(
        partial(second_kernel, order),
        [((2 * slots, patches), BF16), ((n_seq * n_exp, own, width // n_seq), BF16)],
        near,
        far,
        logits,
        tokens_flipped,
        tokens,
        out_grad_flipped,
        limit=12,
    )
    (tok_grad,) = local_call(
        patch_kernel,
        [((patches, width), BF16)],
        weights,
        near,
        far,
        table_near,
        table_far,
        limit=12,
        to_hbm=(0,),
    )

    part = lax.all_to_all(blocks, ("seq", "exp"), 0, 0, tiled=True)
    part = jnp.sum(part.astype(F32), axis=0)
    return (tok_grad, part.T)


def solution(mesh):
    placed = (
        P(("seq", "exp"), None),
        P(None, "exp"),
        P("exp", None, "seq"),
        P("exp", "seq", None),
        P(("seq", "exp"), None),
    )
    return jax.shard_map(
        shards,
        mesh=mesh,
        in_specs=placed,
        out_specs=(P(("seq", "exp"), None), P("seq", "exp")),
        check_vma=False,
    )
```

```python
from functools import partial
import math

import jax
import jax.numpy as jnp
from jax import lax
from jax.experimental import pallas as pl
from jax.experimental.pallas import tpu as pltpu
from jax.sharding import PartitionSpec as P

LANES = 128
F32 = jnp.float32
BF16 = jnp.bfloat16
MIB = 1 << 20


def swap(x, axis, mask):
    return lax.ppermute(x, axis, [(k, k ^ mask) for k in range(lax.axis_size(axis))])


def swaps(parts, axis, masks):
    return [swap(x, axis, mask) for x, mask in zip(parts, masks)]


def to_all(x, axis, masks):
    return swaps([x] * len(masks), axis, masks)


def groups(n, first):
    bits = [1 << k for k in range(n.bit_length() - 1) if 1 << k >= first]
    return [
        [sum(pair), pair[1], pair[0]]
        if len(pair) == 2
        else [pair[0]]
        for pair in (bits[k : k + 2] for k in range(0, len(bits), 2))
    ]


def in_vmem(x):
    return pltpu.with_memory_space_constraint(x, pltpu.VMEM)


def local_call(body, outs, *operands, limit=8, to_hbm=(), loose=(), flops=10**10):
    return pl.pallas_call(
        body,
        out_shape=tuple(
            jax.ShapeDtypeStruct(s, d) if k in to_hbm else pltpu.VMEM(s, d)
            for k, (s, d) in enumerate(outs)
        ),
        in_specs=[pl.BlockSpec(memory_space=pltpu.VMEM)] * len(operands),
        out_specs=tuple(pl.BlockSpec(memory_space=pltpu.VMEM) for _ in outs),
        compiler_params=pltpu.CompilerParams(vmem_limit_bytes=limit * MIB),
        cost_estimate=pl.CostEstimate(flops=flops, bytes_accessed=4 * MIB, transcendentals=0),
    )(*[in_vmem(x) for x in operands])


def product(left, right, over_left, over_right):
    return lax.dot_general(
        left, right, (((over_left,), (over_right,)), ((), ())), preferred_element_type=F32
    )


def rounded(x):
    return x.astype(BF16).astype(F32)


def packed(columns, rows):
    lane = lax.broadcasted_iota(jnp.int32, (rows, LANES), 1)
    out = jnp.zeros((rows, LANES), F32)
    for k, x in enumerate(columns):
        high = rounded(x)
        mid = rounded(x - high)
        for j, piece in enumerate((high, mid, x - high - mid)):
            out = jnp.where(lane == 3 * k + j, piece, out)
    return out


def unpacked(block, count):
    lane = lax.broadcasted_iota(jnp.int32, block.shape, 1)
    return [
        jnp.sum(
            jnp.where((lane >= 3 * k) & (lane < 3 * k + 3), block, 0.0), axis=1, keepdims=True
        )
        for k in range(count)
    ]


def load_kernel(source, out, semaphore):
    copy = pltpu.make_async_copy(source, out, semaphore)
    copy.start()
    copy.wait()


def loaded(x):
    return pl.pallas_call(
        load_kernel,
        out_shape=pltpu.VMEM(x.shape, x.dtype),
        in_specs=[pl.BlockSpec(memory_space=pl.ANY)],
        out_specs=pl.BlockSpec(memory_space=pltpu.VMEM),
        scratch_shapes=[pltpu.SemaphoreType.DMA],
        compiler_params=pltpu.CompilerParams(vmem_limit_bytes=2 * MIB),
        cost_estimate=pl.CostEstimate(flops=10**9, bytes_accessed=2 * x.size, transcendentals=0),
    )(x)


def concat_kernel(*refs):
    out = refs[-1]
    out[...] = jnp.concatenate([r[...].astype(F32) for r in refs[:-1]], axis=0).astype(BF16)


def stack(parts):
    if len(parts) == 1:
        return parts[0]
    rows = sum(p.shape[0] for p in parts)
    return local_call(concat_kernel, [((rows, parts[0].shape[1]), BF16)], *parts)[0]


def softmax_columns(logits):
    weight = jnp.exp(logits - jnp.max(logits, axis=0, keepdims=True))
    return weight / jnp.sum(weight, axis=0, keepdims=True)


def logit_kernel(table, tokens_flipped, tokens_far, logits_out, stats):
    logits = jnp.concatenate(
        [
            product(table[...], tokens_flipped[...], 1, 0),
            product(table[...], tokens_far[...], 1, 1),
        ],
        axis=1,
    )
    logits_out[...] = logits
    top = jnp.max(logits, axis=0, keepdims=True)
    total = jnp.sum(jnp.exp(logits - top), axis=0, keepdims=True)
    row = lax.broadcasted_iota(jnp.int32, stats.shape, 0)
    stats[...] = jnp.where(row == 0, top, jnp.where(row == 1, total, 0.0))


def far_logit_kernel(table, tokens_flipped, out):
    out[...] = product(table[...], tokens_flipped[...], 1, 0)


def dispatch_kernel(logits, tokens, tokens_far, table, sums, stats, table_out):
    table_out[...] = table[...]
    patches = tokens.shape[0]
    top = jnp.max(logits[...], axis=1, keepdims=True)
    weight = jnp.exp(logits[...] - top)
    stats[...] = packed([top, jnp.sum(weight, axis=1, keepdims=True)], stats.shape[0]).astype(BF16)
    weight = weight.astype(BF16)
    both = product(weight[:, :patches], tokens[...], 1, 0)
    both += product(weight[:, patches:], tokens_far[...], 1, 0)
    sums[...] = both.astype(BF16)


def combine_kernel(logits, rows, rows_far, out_grad, out_far, sums, stats, *outs):
    patches, width = out_grad.shape
    other = jnp.concatenate([rows_far[:, patches:], rows_far[:, :patches]], axis=1)
    top = jnp.maximum(rows[:1], other[:1])
    total = rows[1:2] * jnp.exp(rows[:1] - top) + other[1:2] * jnp.exp(other[:1] - top)
    combine = (jnp.exp(logits[...] - top) / total).astype(BF16)
    grads = product(combine[:, :patches], out_grad[...], 1, 0)
    grads += product(combine[:, patches:], out_far[...], 1, 0)
    count = outs[0].shape[0]
    for k, out in enumerate(outs):
        part = slice(k * count, (k + 1) * count)
        out[:, :width] = sums[part].astype(BF16)
        out[:, width : 2 * width] = grads[part].astype(BF16)
        out[:, 2 * width :] = stats[part]


def merged(refs, width):
    stats = [unpacked(r[:, 2 * width :].astype(F32), 2) for r in refs]
    top = stats[0][0]
    for other, _ in stats[1:]:
        top = jnp.maximum(top, other)
    scales = [jnp.exp(t - top) for t, _ in stats]
    total = sum(s * l for s, (_, l) in zip(scales, stats))
    sums = sum(s * r[:, :width].astype(F32) for s, r in zip(scales, refs))
    grads = sum(r[:, width : 2 * width].astype(F32) for r in refs)
    return sums, grads, top, total


def merge_kernel(count, unread, width, *refs):
    sums, grads, top, total = merged(refs[:count], width)
    outs = refs[count + unread :]
    rows = outs[0].shape[0]
    stats = packed([top, total], sums.shape[0])
    for k, out in enumerate(outs):
        part = slice(k * rows, (k + 1) * rows)
        out[:, :width] = sums[part].astype(BF16)
        out[:, width : 2 * width] = grads[part].astype(BF16)
        out[:, 2 * width :] = stats[part].astype(BF16)


def merge(parts, width, pieces, *after):
    rows, columns = parts[0].shape
    return local_call(
        partial(merge_kernel, len(parts), len(after), width),
        [((rows // pieces, columns), BF16)] * pieces,
        *parts,
        *after,
    )


def flip_kernel(index, weight, after, out):
    out[...] = weight[index].T


def flip_whole_kernel(x, out):
    out[...] = x[...].T


def flipped_whole(x):
    shape = (x.shape[1], x.shape[0])
    return local_call(flip_whole_kernel, [(shape, BF16)], x, flops=3 * 10**8)[0]


def flipped(weights, after):
    experts, rows, columns = weights.shape
    return [
        local_call(
            partial(flip_kernel, e), [((columns, rows), BF16)], weights, after, flops=10**9
        )[0]
        for e in range(experts)
    ]


def gelu_and_slope(v):
    root = math.sqrt(2.0 / math.pi)
    t = jnp.tanh(root * (v + 0.044715 * (v * v * v)))
    slope = 0.5 * (1.0 + t) + 0.5 * v * (1.0 - t * t) * (root * (1.0 + 3 * 0.044715 * (v * v)))
    return 0.5 * v * (1.0 + t), slope


def expert_kernel(count, width, *refs):
    parts = refs[:count]
    weight_in, weight_out = refs[count : count + 2]
    experts, _, units = weight_in.shape
    flips = refs[count + 2 : count + 2 + 2 * experts]
    in_flipped, out_flipped = flips[:experts], flips[experts:]
    both, slot_sum, stats = refs[count + 2 + 2 * experts :]
    sums, grads, top, total = merged(parts, width)
    stats[...] = packed([top, total], stats.shape[0])
    sums = sums / total
    slot_sum[...] = sums
    slot_in, grad_out = sums.astype(BF16), grads.astype(BF16)
    rows = sums.shape[0]
    step = min(units, 512)
    row = lax.broadcasted_iota(jnp.int32, (rows, step), 0)
    out_part = jnp.zeros((rows, width), F32)
    in_part = jnp.zeros((rows, width), F32)
    for e in range(experts):
        own = (row >= e * (rows // experts)) & (row < (e + 1) * (rows // experts))
        for c in range(units // step):
            at = slice(c * step, (c + 1) * step)
            pre_act = product(slot_in, weight_in[e, :, at], 1, 0)
            hid_grad = product(grad_out, out_flipped[e][:, at], 1, 0)
            act, slope = gelu_and_slope(pre_act)
            hidden = jnp.where(own, act, 0.0).astype(BF16)
            act_grad = jnp.where(own, hid_grad * slope, 0.0).astype(BF16)
            out_part += product(hidden, weight_out[e, at, :], 1, 0)
            in_part += product(act_grad, in_flipped[e][at, :], 1, 0)
    both[:, :width] = out_part.astype(BF16)
    both[:, width:] = in_part.astype(BF16)


def sum_kernel(count, *refs):
    total = sum(r[...].astype(F32) for r in refs[:count])
    outs = refs[count:]
    rows = outs[0].shape[0]
    for k, out in enumerate(outs):
        out[...] = total[k * rows : (k + 1) * rows].astype(out.dtype)


def sum_of(parts, pieces, dtype):
    rows, columns = parts[0].shape
    return local_call(
        partial(sum_kernel, len(parts)), [((rows // pieces, columns), dtype)] * pieces, *parts
    )


def centre_kernel(count, width, *refs):
    parts = refs[:count]
    slot_sum, stats, _, out = refs[count:]
    total = sum(r[...].astype(F32) for r in parts).astype(BF16)
    grad_in = total[:, width:].astype(F32)
    centre = jnp.sum(slot_sum[...] * grad_in, axis=1, keepdims=True)
    top, denominator = unpacked(stats[...], 2)
    out[:, : 2 * width] = total
    out[:, 2 * width :] = packed([centre, top, denominator], stats.shape[0]).astype(BF16)


def second_kernel(
    order, near, far, logits_near, logits_far, tokens_flipped, tokens, out_grad_flipped, weights, blocks
):
    width = tokens.shape[1]
    half = near.shape[0]

    def against(columns, rows):
        both = jnp.concatenate([near[:, columns], far[:, columns]], axis=0)
        return product(both, rows[...], 1, 0)

    comb_grad = against(slice(0, width), out_grad_flipped)
    disp_grad = against(slice(width, 2 * width), tokens_flipped)
    stats = jnp.concatenate([x[:, 2 * width :].astype(F32) for x in (near, far)], axis=0)
    centre, top, total = unpacked(stats, 3)
    scores = jnp.concatenate([logits_near[:, : tokens.shape[0]], logits_far[...]], axis=0)
    dispatch = jnp.exp(scores - top) / total
    combine = softmax_columns(scores)
    comb_mean = jnp.sum(combine * comb_grad, axis=0, keepdims=True)
    logit_grad = dispatch * (disp_grad - centre) + combine * (comb_grad - comb_mean)
    logit_b = logit_grad.astype(BF16)
    weights[: 2 * half] = dispatch.astype(BF16)
    weights[2 * half :] = logit_b
    part = product(logit_b, tokens[...], 1, 0).astype(BF16)
    me = lax.axis_index("exp")
    n_seq, n_exp = lax.axis_size("seq"), lax.axis_size("exp")
    _, rows, share = blocks.shape
    for k, mask in enumerate(order):
        for s in range(n_seq):
            blocks[s * n_exp + (me ^ mask)] = part[
                k * rows : (k + 1) * rows, s * share : (s + 1) * share
            ]


def patch_kernel(weights, near, far, table_near, table_far, out):
    width = out.shape[1]
    rows = jnp.concatenate(
        [x[:, width : 2 * width] for x in (near, far)] + [table_near[...], table_far[...]], axis=0
    )
    out[...] = product(weights[...], rows, 0, 0).astype(BF16)


def shards(tokens, slot_embed, expert_in, expert_out, out_grad):
    width = tokens.shape[1]
    patches = tokens.shape[0]
    own = slot_embed.shape[1]
    n_exp, n_seq = lax.axis_size("exp"), lax.axis_size("seq")
    slots = own * n_exp
    half = slots // 2
    columns = 2 * width + LANES
    chip_groups = groups(n_exp, 2)
    seq_groups = groups(n_seq, 1)

    def gathered_over_chips(x, here):
        for masks in reversed(chip_groups):
            x = here = stack([here] + to_all(x, "exp", masks))
        return x

    table_near = gathered_over_chips(slot_embed.T, loaded(slot_embed.T))
    tokens_far, out_far = swap(tokens, "exp", 1), swap(out_grad, "exp", 1)

    tokens_flipped, out_grad_flipped = flipped_whole(tokens), flipped_whole(out_grad)
    logits, rows = local_call(
        logit_kernel,
        [((half, 2 * patches), F32), ((8, 2 * patches), F32)],
        table_near,
        tokens_flipped,
        tokens_far,
    )
    sums, stats, table_sent = local_call(
        dispatch_kernel,
        [((half, width), BF16), ((half, LANES), BF16), ((half, width), BF16)],
        logits,
        tokens,
        tokens_far,
        table_near,
        flops=10**9,
    )
    table_far = swap(table_sent, "exp", 1)
    (logits_far,) = local_call(
        far_logit_kernel, [((half, patches), F32)], table_far, tokens_flipped, flops=3 * 10**8
    )
    pieces_first = len(chip_groups[0]) + 1
    pieces = local_call(
        combine_kernel,
        [((half // pieces_first, columns), BF16)] * pieces_first,
        logits,
        rows,
        swap(rows, "exp", 1),
        out_grad,
        out_far,
        sums,
        stats,
        limit=12,
    )
    for k, masks in enumerate(chip_groups):
        if k:
            pieces = merge(parts, width, len(masks) + 1)
        parts = [pieces[0]] + swaps(pieces[1:], "exp", masks)
    own_piece = pieces[0]
    for masks in seq_groups:
        (x,) = merge(parts, width, 1)
        parts = [x] + to_all(x, "seq", masks)
    own_sum = x

    both, slot_sum, stats = local_call(
        partial(expert_kernel, len(parts), width),
        [((own, 2 * width), BF16), ((own, width), F32), ((own, LANES), F32)],
        *parts,
        expert_in,
        expert_out,
        *flipped(expert_in, own_sum),
        *flipped(expert_out, own_piece),
        limit=16,
    )
    parts = [both]
    for k, masks in enumerate(seq_groups):
        if k:
            parts = list(sum_of(parts, 1, BF16))
        parts = parts + to_all(parts[0], "seq", masks)
    (packet,) = local_call(
        partial(centre_kernel, len(parts), width),
        [((own, columns), BF16)],
        *parts,
        slot_sum,
        stats,
        logits_far,
    )
    near = gathered_over_chips(packet, packet)
    far = swap(near, "exp", 1)

    order = [0]
    for masks in reversed(chip_groups):
        order = [r ^ mask for mask in (0, *masks) for r in order]
    order = order + [r ^ 1 for r in order]
    weights, blocks = local_call(
        partial(second_kernel, order),
        [((2 * slots, patches), BF16), ((n_seq * n_exp, own, width // n_seq), BF16)],
        near,
        far,
        logits,
        logits_far,
        tokens_flipped,
        tokens,
        out_grad_flipped,
        limit=12,
    )
    (tok_grad,) = local_call(
        patch_kernel,
        [((patches, width), BF16)],
        weights,
        near,
        far,
        table_near,
        table_far,
        limit=12,
        to_hbm=(0,),
    )

    part = lax.all_to_all(blocks, ("seq", "exp"), 0, 0, tiled=True)
    part = jnp.sum(part.astype(F32), axis=0)
    return (tok_grad, part.T)


def solution(mesh):
    placed = (
        P(("seq", "exp"), None),
        P(None, "exp"),
        P("exp", None, "seq"),
        P("exp", "seq", None),
        P(("seq", "exp"), None),
    )
    return jax.shard_map(
        shards,
        mesh=mesh,
        in_specs=placed,
        out_specs=(P(("seq", "exp"), None), P("seq", "exp")),
        check_vma=False,
    )
```

```python
from functools import partial
import math

import jax
import jax.numpy as jnp
from jax import lax
from jax.experimental import pallas as pl
from jax.experimental.pallas import tpu as pltpu
from jax.sharding import PartitionSpec as P

LANES = 128
F32 = jnp.float32
BF16 = jnp.bfloat16
MIB = 1 << 20


def swap(x, axis, mask):
    return lax.ppermute(x, axis, [(k, k ^ mask) for k in range(lax.axis_size(axis))])


def swaps(parts, axis, masks):
    return [swap(x, axis, mask) for x, mask in zip(parts, masks)]


def to_all(x, axis, masks):
    return swaps([x] * len(masks), axis, masks)


def groups(n, first):
    bits = [1 << k for k in range(n.bit_length() - 1) if 1 << k >= first]
    return [
        [sum(pair), pair[1], pair[0]]
        if len(pair) == 2
        else [pair[0]]
        for pair in (bits[k : k + 2] for k in range(0, len(bits), 2))
    ]


def in_vmem(x):
    return pltpu.with_memory_space_constraint(x, pltpu.VMEM)


def local_call(body, outs, *operands, limit=8, to_hbm=(), loose=(), flops=10**10):
    return pl.pallas_call(
        body,
        out_shape=tuple(
            jax.ShapeDtypeStruct(s, d) if k in to_hbm else pltpu.VMEM(s, d)
            for k, (s, d) in enumerate(outs)
        ),
        in_specs=[pl.BlockSpec(memory_space=pltpu.VMEM)] * len(operands),
        out_specs=tuple(pl.BlockSpec(memory_space=pltpu.VMEM) for _ in outs),
        compiler_params=pltpu.CompilerParams(vmem_limit_bytes=limit * MIB),
        cost_estimate=pl.CostEstimate(flops=flops, bytes_accessed=4 * MIB, transcendentals=0),
    )(*[in_vmem(x) for x in operands])


def product(left, right, over_left, over_right):
    return lax.dot_general(
        left, right, (((over_left,), (over_right,)), ((), ())), preferred_element_type=F32
    )


def rounded(x):
    return x.astype(BF16).astype(F32)


def packed(columns, rows):
    lane = lax.broadcasted_iota(jnp.int32, (rows, LANES), 1)
    out = jnp.zeros((rows, LANES), F32)
    for k, x in enumerate(columns):
        high = rounded(x)
        mid = rounded(x - high)
        for j, piece in enumerate((high, mid, x - high - mid)):
            out = jnp.where(lane == 3 * k + j, piece, out)
    return out


def unpacked(block, count):
    lane = lax.broadcasted_iota(jnp.int32, block.shape, 1)
    return [
        jnp.sum(
            jnp.where((lane >= 3 * k) & (lane < 3 * k + 3), block, 0.0), axis=1, keepdims=True
        )
        for k in range(count)
    ]


def load_kernel(source, out, semaphore):
    copy = pltpu.make_async_copy(source, out, semaphore)
    copy.start()
    copy.wait()


def loaded(x):
    return pl.pallas_call(
        load_kernel,
        out_shape=pltpu.VMEM(x.shape, x.dtype),
        in_specs=[pl.BlockSpec(memory_space=pl.ANY)],
        out_specs=pl.BlockSpec(memory_space=pltpu.VMEM),
        scratch_shapes=[pltpu.SemaphoreType.DMA],
        compiler_params=pltpu.CompilerParams(vmem_limit_bytes=2 * MIB),
        cost_estimate=pl.CostEstimate(flops=10**9, bytes_accessed=2 * x.size, transcendentals=0),
    )(x)


def concat_kernel(*refs):
    out = refs[-1]
    out[...] = jnp.concatenate([r[...].astype(F32) for r in refs[:-1]], axis=0).astype(BF16)


def stack(parts):
    if len(parts) == 1:
        return parts[0]
    rows = sum(p.shape[0] for p in parts)
    return local_call(concat_kernel, [((rows, parts[0].shape[1]), BF16)], *parts)[0]


def softmax_columns(logits):
    weight = jnp.exp(logits - jnp.max(logits, axis=0, keepdims=True))
    return weight / jnp.sum(weight, axis=0, keepdims=True)


def logit_kernel(table, tokens_flipped, tokens_far, logits_out, stats):
    logits = jnp.concatenate(
        [
            product(table[...], tokens_flipped[...], 1, 0),
            product(table[...], tokens_far[...], 1, 1),
        ],
        axis=1,
    )
    logits_out[...] = logits
    top = jnp.max(logits, axis=0, keepdims=True)
    total = jnp.sum(jnp.exp(logits - top), axis=0, keepdims=True)
    row = lax.broadcasted_iota(jnp.int32, stats.shape, 0)
    stats[...] = jnp.where(row == 0, top, jnp.where(row == 1, total, 0.0))


def dispatch_kernel(logits, tokens, tokens_far, table, sums, stats, table_out):
    table_out[...] = table[...]
    patches = tokens.shape[0]
    top = jnp.max(logits[...], axis=1, keepdims=True)
    weight = jnp.exp(logits[...] - top)
    stats[...] = packed([top, jnp.sum(weight, axis=1, keepdims=True)], stats.shape[0]).astype(BF16)
    weight = weight.astype(BF16)
    both = product(weight[:, :patches], tokens[...], 1, 0)
    both += product(weight[:, patches:], tokens_far[...], 1, 0)
    sums[...] = both.astype(BF16)


def as_here(rows_far):
    half = rows_far.shape[1] // 2
    return jnp.concatenate([rows_far[:, half:], rows_far[:, :half]], axis=1)


def combine_weights(logits, rows, rows_far):
    other = as_here(rows_far)
    top = jnp.maximum(rows[:1], other[:1])
    total = rows[1:2] * jnp.exp(rows[:1] - top) + other[1:2] * jnp.exp(other[:1] - top)
    return jnp.exp(logits[...] - top) / total


def combine_kernel(logits, rows, rows_far, out_grad, out_far, sums, stats, *outs):
    patches, width = out_grad.shape
    combine = combine_weights(logits, rows, rows_far).astype(BF16)
    grads = product(combine[:, :patches], out_grad[...], 1, 0)
    grads += product(combine[:, patches:], out_far[...], 1, 0)
    count = outs[0].shape[0]
    for k, out in enumerate(outs):
        part = slice(k * count, (k + 1) * count)
        out[:, :width] = sums[part].astype(BF16)
        out[:, width : 2 * width] = grads[part].astype(BF16)
        out[:, 2 * width :] = stats[part]


def merged(refs, width):
    stats = [unpacked(r[:, 2 * width :].astype(F32), 2) for r in refs]
    top = stats[0][0]
    for other, _ in stats[1:]:
        top = jnp.maximum(top, other)
    scales = [jnp.exp(t - top) for t, _ in stats]
    total = sum(s * l for s, (_, l) in zip(scales, stats))
    sums = sum(s * r[:, :width].astype(F32) for s, r in zip(scales, refs))
    grads = sum(r[:, width : 2 * width].astype(F32) for r in refs)
    return sums, grads, top, total


def merge_kernel(count, unread, width, *refs):
    sums, grads, top, total = merged(refs[:count], width)
    outs = refs[count + unread :]
    rows = outs[0].shape[0]
    stats = packed([top, total], sums.shape[0])
    for k, out in enumerate(outs):
        part = slice(k * rows, (k + 1) * rows)
        out[:, :width] = sums[part].astype(BF16)
        out[:, width : 2 * width] = grads[part].astype(BF16)
        out[:, 2 * width :] = stats[part].astype(BF16)


def merge(parts, width, pieces, *after):
    rows, columns = parts[0].shape
    return local_call(
        partial(merge_kernel, len(parts), len(after), width),
        [((rows // pieces, columns), BF16)] * pieces,
        *parts,
        *after,
    )


def flip_kernel(index, weight, after, out):
    out[...] = weight[index].T


def flip_whole_kernel(x, out):
    out[...] = x[...].T


def flipped_whole(x):
    shape = (x.shape[1], x.shape[0])
    return local_call(flip_whole_kernel, [(shape, BF16)], x, flops=3 * 10**8)[0]


def flipped(weights, after):
    experts, rows, columns = weights.shape
    return [
        local_call(
            partial(flip_kernel, e), [((columns, rows), BF16)], weights, after, flops=10**9
        )[0]
        for e in range(experts)
    ]


def gelu_and_slope(v):
    root = math.sqrt(2.0 / math.pi)
    t = jnp.tanh(root * (v + 0.044715 * (v * v * v)))
    slope = 0.5 * (1.0 + t) + 0.5 * v * (1.0 - t * t) * (root * (1.0 + 3 * 0.044715 * (v * v)))
    return 0.5 * v * (1.0 + t), slope


def expert_kernel(count, width, *refs):
    parts = refs[:count]
    weight_in, weight_out = refs[count : count + 2]
    experts, _, units = weight_in.shape
    flips = refs[count + 2 : count + 2 + 2 * experts]
    in_flipped, out_flipped = flips[:experts], flips[experts:]
    both, slot_sum, stats = refs[count + 2 + 2 * experts :]
    sums, grads, top, total = merged(parts, width)
    stats[...] = packed([top, total], stats.shape[0])
    sums = sums / total
    slot_sum[...] = sums
    slot_in, grad_out = sums.astype(BF16), grads.astype(BF16)
    rows = sums.shape[0]
    step = min(units, 512)
    row = lax.broadcasted_iota(jnp.int32, (rows, step), 0)
    out_part = jnp.zeros((rows, width), F32)
    in_part = jnp.zeros((rows, width), F32)
    for e in range(experts):
        own = (row >= e * (rows // experts)) & (row < (e + 1) * (rows // experts))
        for c in range(units // step):
            at = slice(c * step, (c + 1) * step)
            pre_act = product(slot_in, weight_in[e, :, at], 1, 0)
            hid_grad = product(grad_out, out_flipped[e][:, at], 1, 0)
            act, slope = gelu_and_slope(pre_act)
            hidden = jnp.where(own, act, 0.0).astype(BF16)
            act_grad = jnp.where(own, hid_grad * slope, 0.0).astype(BF16)
            out_part += product(hidden, weight_out[e, at, :], 1, 0)
            in_part += product(act_grad, in_flipped[e][at, :], 1, 0)
    both[:, :width] = out_part.astype(BF16)
    both[:, width:] = in_part.astype(BF16)


def sum_kernel(count, *refs):
    total = sum(r[...].astype(F32) for r in refs[:count])
    outs = refs[count:]
    rows = outs[0].shape[0]
    for k, out in enumerate(outs):
        out[...] = total[k * rows : (k + 1) * rows].astype(out.dtype)


def sum_of(parts, pieces, dtype):
    rows, columns = parts[0].shape
    return local_call(
        partial(sum_kernel, len(parts)), [((rows // pieces, columns), dtype)] * pieces, *parts
    )


def centre_kernel(count, width, *refs):
    parts = refs[:count]
    slot_sum, stats, _, out = refs[count:]
    total = sum(r[...].astype(F32) for r in parts).astype(BF16)
    grad_in = total[:, width:].astype(F32)
    centre = jnp.sum(slot_sum[...] * grad_in, axis=1, keepdims=True)
    top, denominator = unpacked(stats[...], 2)
    out[:, : 2 * width] = total
    out[:, 2 * width :] = packed([centre, top, denominator], stats.shape[0]).astype(BF16)


def grad_kernel(
    near,
    logits,
    rows,
    rows_far,
    tokens_flipped,
    tokens_far,
    out_grad_flipped,
    out_far,
    direct,
    combine_out,
    dispatch_out,
    mean,
):
    width = tokens_flipped.shape[0]

    def against(columns, flipped_here, far):
        left = near[:, columns]
        return jnp.concatenate(
            [product(left, flipped_here[...], 1, 0), product(left, far[...], 1, 1)], axis=1
        )

    comb_grad = against(slice(0, width), out_grad_flipped, out_far)
    disp_grad = against(slice(width, 2 * width), tokens_flipped, tokens_far)
    centre, top, total = unpacked(near[:, 2 * width :].astype(F32), 3)
    dispatch = jnp.exp(logits[...] - top) / total
    combine = combine_weights(logits, rows, rows_far)
    weighted = combine * comb_grad
    direct[...] = dispatch * (disp_grad - centre) + weighted
    combine_out[...] = combine
    dispatch_out[...] = dispatch
    row = lax.broadcasted_iota(jnp.int32, mean.shape, 0)
    mean[...] = jnp.where(row == 0, jnp.sum(weighted, axis=0, keepdims=True), 0.0)


def block_kernel(
    order,
    direct,
    combine,
    dispatch,
    mean,
    mean_far,
    tokens,
    tokens_far,
    weights,
    weights_sent,
    blocks,
):
    patches, width = tokens.shape
    half = direct.shape[0]
    comb_mean = mean[:1] + as_here(mean_far)[:1]
    logit_grad = direct[...] - combine[...] * comb_mean
    logit_b = logit_grad.astype(BF16)
    part = product(logit_b[:, :patches], tokens[...], 1, 0)
    part += product(logit_b[:, patches:], tokens_far[...], 1, 0)
    part = part.astype(BF16)
    for out, at in ((weights, slice(0, patches)), (weights_sent, slice(patches, 2 * patches))):
        out[:half] = dispatch[:, at].astype(BF16)
        out[half:] = logit_b[:, at]
    chip = lax.axis_index("exp") // 2
    n_seq, n_chips = lax.axis_size("seq"), lax.axis_size("exp") // 2
    _, rows, share = blocks.shape
    for k, mask in enumerate(order):
        for s in range(n_seq):
            blocks[s * n_chips + (chip ^ mask)] = part[
                k * rows : (k + 1) * rows, s * share : (s + 1) * share
            ]


def grad_part_kernel(near, after, out):
    width = out.shape[1]
    out[...] = near[:, width : 2 * width]


def patch_kernel(weights, weights_far, near, table, grad_far, table_far, out):
    width = out.shape[1]
    left = jnp.concatenate([weights[...], weights_far[...]], axis=0)
    rows = jnp.concatenate(
        [near[:, width : 2 * width], table[...], grad_far[...], table_far[...]], axis=0
    )
    out[...] = product(left, rows, 0, 0).astype(BF16)


def shards(tokens, slot_embed, expert_in, expert_out, out_grad):
    width = tokens.shape[1]
    patches = tokens.shape[0]
    own = slot_embed.shape[1]
    n_exp, n_seq = lax.axis_size("exp"), lax.axis_size("seq")
    slots = own * n_exp
    half = slots // 2
    columns = 2 * width + LANES
    chip_groups = groups(n_exp, 2)
    seq_groups = groups(n_seq, 1)

    def gathered_over_chips(x, here):
        for masks in reversed(chip_groups):
            x = here = stack([here] + to_all(x, "exp", masks))
        return x

    table_near = gathered_over_chips(slot_embed.T, loaded(slot_embed.T))
    tokens_far, out_far = swap(tokens, "exp", 1), swap(out_grad, "exp", 1)

    tokens_flipped, out_grad_flipped = flipped_whole(tokens), flipped_whole(out_grad)
    logits, rows = local_call(
        logit_kernel,
        [((half, 2 * patches), F32), ((8, 2 * patches), F32)],
        table_near,
        tokens_flipped,
        tokens_far,
    )
    sums, stats, table_sent = local_call(
        dispatch_kernel,
        [((half, width), BF16), ((half, LANES), BF16), ((half, width), BF16)],
        logits,
        tokens,
        tokens_far,
        table_near,
        flops=10**9,
    )
    table_far = swap(table_sent, "exp", 1)
    pieces_first = len(chip_groups[0]) + 1
    rows_far = swap(rows, "exp", 1)
    pieces = local_call(
        combine_kernel,
        [((half // pieces_first, columns), BF16)] * pieces_first,
        logits,
        rows,
        rows_far,
        out_grad,
        out_far,
        sums,
        stats,
        limit=12,
    )
    for k, masks in enumerate(chip_groups):
        if k:
            pieces = merge(parts, width, len(masks) + 1)
        parts = [pieces[0]] + swaps(pieces[1:], "exp", masks)
    own_piece = pieces[0]
    for masks in seq_groups:
        (x,) = merge(parts, width, 1)
        parts = [x] + to_all(x, "seq", masks)
    own_sum = x

    both, slot_sum, stats = local_call(
        partial(expert_kernel, len(parts), width),
        [((own, 2 * width), BF16), ((own, width), F32), ((own, LANES), F32)],
        *parts,
        expert_in,
        expert_out,
        *flipped(expert_in, own_sum),
        *flipped(expert_out, own_piece),
        limit=16,
    )
    parts = [both]
    for k, masks in enumerate(seq_groups):
        if k:
            parts = list(sum_of(parts, 1, BF16))
        parts = parts + to_all(parts[0], "seq", masks)
    (packet,) = local_call(
        partial(centre_kernel, len(parts), width),
        [((own, columns), BF16)],
        *parts,
        slot_sum,
        stats,
        table_far,
    )
    near = gathered_over_chips(packet, packet)
    direct, combine, dispatch, mean = local_call(
        grad_kernel,
        [((half, 2 * patches), F32)] * 3 + [((8, 2 * patches), F32)],
        near,
        logits,
        rows,
        rows_far,
        tokens_flipped,
        tokens_far,
        out_grad_flipped,
        out_far,
        limit=12,
    )
    order = [0]
    for masks in reversed(chip_groups):
        order = [r ^ (mask // 2) for mask in (0, *masks) for r in order]
    (grad_sent,) = local_call(
        grad_part_kernel, [((half, width), BF16)], near, mean, flops=10**8
    )
    weights, weights_sent, blocks = local_call(
        partial(block_kernel, order),
        [((2 * half, patches), BF16)] * 2
        + [((n_seq * n_exp // 2, own, width // n_seq), BF16)],
        direct,
        combine,
        dispatch,
        mean,
        swap(mean, "exp", 1),
        tokens,
        tokens_far,
        limit=12,
    )
    (tok_grad,) = local_call(
        patch_kernel,
        [((patches, width), BF16)],
        weights,
        swap(weights_sent, "exp", 1),
        near,
        table_near,
        swap(grad_sent, "exp", 1),
        table_far,
        limit=12,
        to_hbm=(0,),
    )
    same_core = [
        [s * n_exp + 2 * chip + core for s in range(n_seq) for chip in range(n_exp // 2)]
        for core in range(2)
    ]
    part = lax.all_to_all(
        blocks, ("seq", "exp"), 0, 0, tiled=True, axis_index_groups=same_core
    )
    part = jnp.sum(part.astype(F32), axis=0)
    return (tok_grad, part.T)


def solution(mesh):
    placed = (
        P(("seq", "exp"), None),
        P(None, "exp"),
        P("exp", None, "seq"),
        P("exp", "seq", None),
        P(("seq", "exp"), None),
    )
    return jax.shard_map(
        shards,
        mesh=mesh,
        in_specs=placed,
        out_specs=(P(("seq", "exp"), None), P("seq", "exp")),
        check_vma=False,
    )
```

```python
from functools import partial
import math

import jax
import jax.numpy as jnp
from jax import lax
from jax.experimental import pallas as pl
from jax.experimental.pallas import tpu as pltpu
from jax.sharding import PartitionSpec as P

LANES = 128
F32 = jnp.float32
BF16 = jnp.bfloat16
MIB = 1 << 20


def swap(x, axis, mask):
    return lax.ppermute(x, axis, [(k, k ^ mask) for k in range(lax.axis_size(axis))])


def swaps(parts, axis, masks):
    return [swap(x, axis, mask) for x, mask in zip(parts, masks)]


def to_all(x, axis, masks):
    return swaps([x] * len(masks), axis, masks)


def groups(n, first):
    bits = [1 << k for k in range(n.bit_length() - 1) if 1 << k >= first]
    return [
        [pair[1], sum(pair), pair[0]] if first > 1 else [sum(pair), pair[1], pair[0]]
        if len(pair) == 2
        else [pair[0]]
        for pair in (bits[k : k + 2] for k in range(0, len(bits), 2))
    ]


def in_vmem(x):
    return pltpu.with_memory_space_constraint(x, pltpu.VMEM)


def local_call(body, outs, *operands, limit=8, to_hbm=(), loose=(), flops=10**10):
    return pl.pallas_call(
        body,
        out_shape=tuple(
            jax.ShapeDtypeStruct(s, d) if k in to_hbm else pltpu.VMEM(s, d)
            for k, (s, d) in enumerate(outs)
        ),
        in_specs=[pl.BlockSpec(memory_space=pltpu.VMEM)] * len(operands),
        out_specs=tuple(pl.BlockSpec(memory_space=pltpu.VMEM) for _ in outs),
        compiler_params=pltpu.CompilerParams(vmem_limit_bytes=limit * MIB),
        cost_estimate=pl.CostEstimate(flops=flops, bytes_accessed=4 * MIB, transcendentals=0),
    )(*[in_vmem(x) for x in operands])


def product(left, right, over_left, over_right):
    return lax.dot_general(
        left, right, (((over_left,), (over_right,)), ((), ())), preferred_element_type=F32
    )


def rounded(x):
    return x.astype(BF16).astype(F32)


def packed(columns, rows):
    lane = lax.broadcasted_iota(jnp.int32, (rows, LANES), 1)
    out = jnp.zeros((rows, LANES), F32)
    for k, x in enumerate(columns):
        high = rounded(x)
        mid = rounded(x - high)
        for j, piece in enumerate((high, mid, x - high - mid)):
            out = jnp.where(lane == 3 * k + j, piece, out)
    return out


def unpacked(block, count):
    lane = lax.broadcasted_iota(jnp.int32, block.shape, 1)
    return [
        jnp.sum(
            jnp.where((lane >= 3 * k) & (lane < 3 * k + 3), block, 0.0), axis=1, keepdims=True
        )
        for k in range(count)
    ]


def plain_copy_kernel(x, out):
    out[...] = x[...]


def loaded(x):
    return local_call(plain_copy_kernel, [(x.shape, x.dtype)], x, limit=2, flops=10**9)[0]


def concat_kernel(*refs):
    out = refs[-1]
    out[...] = jnp.concatenate([r[...].astype(F32) for r in refs[:-1]], axis=0).astype(BF16)


def stack(parts):
    if len(parts) == 1:
        return parts[0]
    rows = sum(p.shape[0] for p in parts)
    return local_call(concat_kernel, [((rows, parts[0].shape[1]), BF16)], *parts)[0]


def softmax_columns(logits):
    weight = jnp.exp(logits - jnp.max(logits, axis=0, keepdims=True))
    return weight / jnp.sum(weight, axis=0, keepdims=True)


def logit_kernel(table, tokens_flipped, tokens_far, logits_out, stats):
    logits = jnp.concatenate(
        [
            product(table[...], tokens_flipped[...], 1, 0),
            product(table[...], tokens_far[...], 1, 1),
        ],
        axis=1,
    )
    logits_out[...] = logits
    top = jnp.max(logits, axis=0, keepdims=True)
    total = jnp.sum(jnp.exp(logits - top), axis=0, keepdims=True)
    row = lax.broadcasted_iota(jnp.int32, stats.shape, 0)
    stats[...] = jnp.where(row == 0, top, jnp.where(row == 1, total, 0.0))


def dispatch_kernel(logits, tokens, tokens_far, sums, stats):
    patches = tokens.shape[0]
    top = jnp.max(logits[...], axis=1, keepdims=True)
    weight = jnp.exp(logits[...] - top)
    stats[...] = packed([top, jnp.sum(weight, axis=1, keepdims=True)], stats.shape[0]).astype(BF16)
    weight = weight.astype(BF16)
    both = product(weight[:, :patches], tokens[...], 1, 0)
    both += product(weight[:, patches:], tokens_far[...], 1, 0)
    sums[...] = both.astype(BF16)


def as_here(rows_far):
    half = rows_far.shape[1] // 2
    return jnp.concatenate([rows_far[:, half:], rows_far[:, :half]], axis=1)


def combine_weights(logits, rows, rows_far):
    other = as_here(rows_far)
    top = jnp.maximum(rows[:1], other[:1])
    total = rows[1:2] * jnp.exp(rows[:1] - top) + other[1:2] * jnp.exp(other[:1] - top)
    return jnp.exp(logits[...] - top) / total


def combine_kernel(logits, rows, rows_far, out_grad, out_far, sums, stats, *outs):
    patches, width = out_grad.shape
    combine = combine_weights(logits, rows, rows_far).astype(BF16)
    grads = product(combine[:, :patches], out_grad[...], 1, 0)
    grads += product(combine[:, patches:], out_far[...], 1, 0)
    count = outs[0].shape[0]
    for k, out in enumerate(outs):
        part = slice(k * count, (k + 1) * count)
        out[:, :width] = sums[part].astype(BF16)
        out[:, width : 2 * width] = grads[part].astype(BF16)
        out[:, 2 * width :] = stats[part]


def merged(refs, width):
    stats = [unpacked(r[:, 2 * width :].astype(F32), 2) for r in refs]
    top = stats[0][0]
    for other, _ in stats[1:]:
        top = jnp.maximum(top, other)
    scales = [jnp.exp(t - top) for t, _ in stats]
    total = sum(s * l for s, (_, l) in zip(scales, stats))
    sums = sum(s * r[:, :width].astype(F32) for s, r in zip(scales, refs))
    grads = sum(r[:, width : 2 * width].astype(F32) for r in refs)
    return sums, grads, top, total


def merge_kernel(count, unread, width, *refs):
    sums, grads, top, total = merged(refs[:count], width)
    outs = refs[count + unread :]
    rows = outs[0].shape[0]
    stats = packed([top, total], sums.shape[0])
    for k, out in enumerate(outs):
        part = slice(k * rows, (k + 1) * rows)
        out[:, :width] = sums[part].astype(BF16)
        out[:, width : 2 * width] = grads[part].astype(BF16)
        out[:, 2 * width :] = stats[part].astype(BF16)


def merge(parts, width, pieces, *after):
    rows, columns = parts[0].shape
    return local_call(
        partial(merge_kernel, len(parts), len(after), width),
        [((rows // pieces, columns), BF16)] * pieces,
        *parts,
        *after,
    )


def flip_kernel(index, weight, after, out):
    out[...] = weight[index].T


def flip_whole_kernel(x, out):
    out[...] = x[...].T


def flipped_whole(x):
    shape = (x.shape[1], x.shape[0])
    return local_call(flip_whole_kernel, [(shape, BF16)], x, flops=3 * 10**8)[0]


def flipped(weights, after):
    experts, rows, columns = weights.shape
    return [
        local_call(
            partial(flip_kernel, e), [((columns, rows), BF16)], weights, after, flops=10**9
        )[0]
        for e in range(experts)
    ]


def gelu_and_slope(v):
    root = math.sqrt(2.0 / math.pi)
    t = jnp.tanh(root * (v + 0.044715 * (v * v * v)))
    slope = 0.5 * (1.0 + t) + 0.5 * v * (1.0 - t * t) * (root * (1.0 + 3 * 0.044715 * (v * v)))
    return 0.5 * v * (1.0 + t), slope


def expert_kernel(count, width, *refs):
    parts = refs[:count]
    weight_in, weight_out = refs[count : count + 2]
    experts, _, units = weight_in.shape
    flips = refs[count + 2 : count + 2 + 2 * experts]
    in_flipped, out_flipped = flips[:experts], flips[experts:]
    both, slot_sum, stats = refs[count + 2 + 2 * experts :]
    sums, grads, top, total = merged(parts, width)
    stats[...] = packed([top, total], stats.shape[0])
    sums = sums / total
    slot_sum[...] = sums
    slot_in, grad_out = sums.astype(BF16), grads.astype(BF16)
    rows = sums.shape[0]
    step = min(units, 512)
    row = lax.broadcasted_iota(jnp.int32, (rows, step), 0)
    out_part = jnp.zeros((rows, width), F32)
    in_part = jnp.zeros((rows, width), F32)
    for e in range(experts):
        own = (row >= e * (rows // experts)) & (row < (e + 1) * (rows // experts))
        for c in range(units // step):
            at = slice(c * step, (c + 1) * step)
            pre_act = product(slot_in, weight_in[e, :, at], 1, 0)
            hid_grad = product(grad_out, out_flipped[e][:, at], 1, 0)
            act, slope = gelu_and_slope(pre_act)
            hidden = jnp.where(own, act, 0.0).astype(BF16)
            act_grad = jnp.where(own, hid_grad * slope, 0.0).astype(BF16)
            out_part += product(hidden, weight_out[e, at, :], 1, 0)
            in_part += product(act_grad, in_flipped[e][at, :], 1, 0)
    both[:, :width] = out_part.astype(BF16)
    both[:, width:] = in_part.astype(BF16)


def sum_kernel(count, *refs):
    total = sum(r[...].astype(F32) for r in refs[:count])
    outs = refs[count:]
    rows = outs[0].shape[0]
    for k, out in enumerate(outs):
        out[...] = total[k * rows : (k + 1) * rows].astype(out.dtype)


def sum_of(parts, pieces, dtype):
    rows, columns = parts[0].shape
    return local_call(
        partial(sum_kernel, len(parts)), [((rows // pieces, columns), dtype)] * pieces, *parts
    )


def centre_kernel(count, width, *refs):
    parts = refs[:count]
    slot_sum, stats, out = refs[count:]
    total = sum(r[...].astype(F32) for r in parts).astype(BF16)
    grad_in = total[:, width:].astype(F32)
    centre = jnp.sum(slot_sum[...] * grad_in, axis=1, keepdims=True)
    top, denominator = unpacked(stats[...], 2)
    out[:, : 2 * width] = total
    out[:, 2 * width :] = packed([centre, top, denominator], stats.shape[0]).astype(BF16)


def grad_kernel(
    near,
    logits,
    rows,
    rows_far,
    tokens_flipped,
    tokens_far,
    out_grad_flipped,
    out_far,
    direct,
    combine_out,
    dispatch_out,
    mean,
):
    width = tokens_flipped.shape[0]

    def against(columns, flipped_here, far):
        left = near[:, columns]
        return jnp.concatenate(
            [product(left, flipped_here[...], 1, 0), product(left, far[...], 1, 1)], axis=1
        )

    comb_grad = against(slice(0, width), out_grad_flipped, out_far)
    disp_grad = against(slice(width, 2 * width), tokens_flipped, tokens_far)
    centre, top, total = unpacked(near[:, 2 * width :].astype(F32), 3)
    dispatch = jnp.exp(logits[...] - top) / total
    combine = combine_weights(logits, rows, rows_far)
    weighted = combine * comb_grad
    direct[...] = dispatch * (disp_grad - centre) + weighted
    combine_out[...] = combine
    dispatch_out[...] = dispatch
    row = lax.broadcasted_iota(jnp.int32, mean.shape, 0)
    mean[...] = jnp.where(row == 0, jnp.sum(weighted, axis=0, keepdims=True), 0.0)


def block_kernel(
    order,
    direct,
    combine,
    dispatch,
    mean,
    mean_far,
    tokens,
    tokens_far,
    weights,
    weights_sent,
    blocks,
):
    patches, width = tokens.shape
    half = direct.shape[0]
    comb_mean = mean[:1] + as_here(mean_far)[:1]
    logit_grad = direct[...] - combine[...] * comb_mean
    logit_b = logit_grad.astype(BF16)
    part = product(logit_b[:, :patches], tokens[...], 1, 0)
    part += product(logit_b[:, patches:], tokens_far[...], 1, 0)
    part = part.astype(BF16)
    for out, at in ((weights, slice(0, patches)), (weights_sent, slice(patches, 2 * patches))):
        out[:half] = dispatch[:, at].astype(BF16)
        out[half:] = logit_b[:, at]
    chip = lax.axis_index("exp") // 2
    n_seq, n_chips = lax.axis_size("seq"), lax.axis_size("exp") // 2
    _, rows, share = blocks.shape
    for k, mask in enumerate(order):
        for s in range(n_seq):
            blocks[s * n_chips + (chip ^ mask)] = part[
                k * rows : (k + 1) * rows, s * share : (s + 1) * share
            ]


def grad_part_kernel(near, after, out):
    width = out.shape[1]
    out[...] = near[:, width : 2 * width]


def copy_kernel(x, after, out):
    out[...] = x[...]


def patch_kernel(weights, weights_far, near, table, grad_far, table_far, out):
    width = out.shape[1]
    left = jnp.concatenate([weights[...], weights_far[...]], axis=0)
    rows = jnp.concatenate(
        [near[:, width : 2 * width], table[...], grad_far[...], table_far[...]], axis=0
    )
    out[...] = product(left, rows, 0, 0).astype(BF16)


def shards(tokens, slot_embed, expert_in, expert_out, out_grad):
    width = tokens.shape[1]
    patches = tokens.shape[0]
    own = slot_embed.shape[1]
    n_exp, n_seq = lax.axis_size("exp"), lax.axis_size("seq")
    slots = own * n_exp
    half = slots // 2
    columns = 2 * width + LANES
    chip_groups = groups(n_exp, 2)
    seq_groups = groups(n_seq, 1)

    def gathered_over_chips(x, here):
        for masks in reversed(chip_groups):
            x = here = stack([here] + to_all(x, "exp", masks))
        return x

    table_near = gathered_over_chips(slot_embed.T, loaded(slot_embed.T))
    tokens_far, out_far = swap(tokens, "exp", 1), swap(out_grad, "exp", 1)

    tokens_flipped, out_grad_flipped = flipped_whole(tokens), flipped_whole(out_grad)
    logits, rows = local_call(
        logit_kernel,
        [((half, 2 * patches), F32), ((8, 2 * patches), F32)],
        table_near,
        tokens_flipped,
        tokens_far,
    )
    sums, stats = local_call(
        dispatch_kernel,
        [((half, width), BF16), ((half, LANES), BF16)],
        logits,
        tokens,
        tokens_far,
        flops=10**9,
    )
    pieces_first = len(chip_groups[0]) + 1
    rows_far = swap(rows, "exp", 1)
    pieces = local_call(
        combine_kernel,
        [((half // pieces_first, columns), BF16)] * pieces_first,
        logits,
        rows,
        rows_far,
        out_grad,
        out_far,
        sums,
        stats,
        limit=12,
    )
    for k, masks in enumerate(chip_groups):
        if k:
            pieces = merge(parts, width, len(masks) + 1)
        parts = [pieces[0]] + swaps(pieces[1:], "exp", masks)
    own_piece = pieces[0]
    for masks in seq_groups:
        (x,) = merge(parts, width, 1)
        parts = [x] + to_all(x, "seq", masks)
    own_sum = x

    both, slot_sum, stats = local_call(
        partial(expert_kernel, len(parts), width),
        [((own, 2 * width), BF16), ((own, width), F32), ((own, LANES), F32)],
        *parts,
        expert_in,
        expert_out,
        *flipped(expert_in, own_sum),
        *flipped(expert_out, own_piece),
        limit=16,
    )
    parts = [both]
    for k, masks in enumerate(seq_groups):
        if k:
            parts = list(sum_of(parts, 1, BF16))
        parts = parts + to_all(parts[0], "seq", masks)
    (packet,) = local_call(
        partial(centre_kernel, len(parts), width),
        [((own, columns), BF16)],
        *parts,
        slot_sum,
        stats,
    )
    (table_sent,) = local_call(
        copy_kernel, [((half, width), BF16)], table_near, packet, flops=10**8
    )
    table_far = swap(table_sent, "exp", 1)
    near = gathered_over_chips(packet, packet)
    direct, combine, dispatch, mean = local_call(
        grad_kernel,
        [((half, 2 * patches), F32)] * 3 + [((8, 2 * patches), F32)],
        near,
        logits,
        rows,
        rows_far,
        tokens_flipped,
        tokens_far,
        out_grad_flipped,
        out_far,
        limit=12,
    )
    order = [0]
    for masks in reversed(chip_groups):
        order = [r ^ (mask // 2) for mask in (0, *masks) for r in order]
    (grad_sent,) = local_call(
        grad_part_kernel, [((half, width), BF16)], near, mean, flops=10**8
    )
    weights, weights_sent, blocks = local_call(
        partial(block_kernel, order),
        [((2 * half, patches), BF16)] * 2
        + [((n_seq * n_exp // 2, own, width // n_seq), BF16)],
        direct,
        combine,
        dispatch,
        mean,
        swap(mean, "exp", 1),
        tokens,
        tokens_far,
        limit=12,
    )
    (tok_grad,) = local_call(
        patch_kernel,
        [((patches, width), BF16)],
        weights,
        swap(weights_sent, "exp", 1),
        near,
        table_near,
        swap(grad_sent, "exp", 1),
        table_far,
        limit=12,
        to_hbm=(0,),
    )
    same_core = [
        [s * n_exp + 2 * chip + core for s in range(n_seq) for chip in range(n_exp // 2)]
        for core in range(2)
    ]
    part = lax.all_to_all(
        blocks, ("seq", "exp"), 0, 0, tiled=True, axis_index_groups=same_core
    )
    part = jnp.sum(part.astype(F32), axis=0)
    return (tok_grad, part.T)


def solution(mesh):
    placed = (
        P(("seq", "exp"), None),
        P(None, "exp"),
        P("exp", None, "seq"),
        P("exp", "seq", None),
        P(("seq", "exp"), None),
    )
    return jax.shard_map(
        shards,
        mesh=mesh,
        in_specs=placed,
        out_specs=(P(("seq", "exp"), None), P("seq", "exp")),
        check_vma=False,
    )
```

```python
from functools import partial
import math

import jax
import jax.numpy as jnp
from jax import lax
from jax.experimental import pallas as pl
from jax.experimental.pallas import tpu as pltpu
from jax.sharding import PartitionSpec as P

LANES = 128
F32 = jnp.float32
BF16 = jnp.bfloat16
MIB = 1 << 20


def swap(x, axis, mask):
    return lax.ppermute(x, axis, [(k, k ^ mask) for k in range(lax.axis_size(axis))])


def swaps(parts, axis, masks):
    return [swap(x, axis, mask) for x, mask in zip(parts, masks)]


def to_all(x, axis, masks):
    return swaps([x] * len(masks), axis, masks)


def groups(n, first):
    bits = [1 << k for k in range(n.bit_length() - 1) if 1 << k >= first]
    return [
        [pair[1], sum(pair), pair[0]] if first > 1 else [sum(pair), pair[1], pair[0]]
        if len(pair) == 2
        else [pair[0]]
        for pair in (bits[k : k + 2] for k in range(0, len(bits), 2))
    ]


def in_vmem(x):
    return pltpu.with_memory_space_constraint(x, pltpu.VMEM)


def local_call(body, outs, *operands, limit=8, to_hbm=(), loose=(), flops=10**10):
    return pl.pallas_call(
        body,
        out_shape=tuple(
            jax.ShapeDtypeStruct(s, d) if k in to_hbm else pltpu.VMEM(s, d)
            for k, (s, d) in enumerate(outs)
        ),
        in_specs=[pl.BlockSpec(memory_space=pltpu.VMEM)] * len(operands),
        out_specs=tuple(pl.BlockSpec(memory_space=pltpu.VMEM) for _ in outs),
        compiler_params=pltpu.CompilerParams(vmem_limit_bytes=limit * MIB),
        cost_estimate=pl.CostEstimate(flops=flops, bytes_accessed=4 * MIB, transcendentals=0),
    )(*[in_vmem(x) for x in operands])


def product(left, right, over_left, over_right):
    return lax.dot_general(
        left, right, (((over_left,), (over_right,)), ((), ())), preferred_element_type=F32
    )


def rounded(x):
    return x.astype(BF16).astype(F32)


def packed(columns, rows):
    lane = lax.broadcasted_iota(jnp.int32, (rows, LANES), 1)
    out = jnp.zeros((rows, LANES), F32)
    for k, x in enumerate(columns):
        high = rounded(x)
        mid = rounded(x - high)
        for j, piece in enumerate((high, mid, x - high - mid)):
            out = jnp.where(lane == 3 * k + j, piece, out)
    return out


def unpacked(block, count):
    lane = lax.broadcasted_iota(jnp.int32, block.shape, 1)
    return [
        jnp.sum(
            jnp.where((lane >= 3 * k) & (lane < 3 * k + 3), block, 0.0), axis=1, keepdims=True
        )
        for k in range(count)
    ]


def plain_copy_kernel(x, out):
    out[...] = x[...]


def loaded(x):
    return local_call(plain_copy_kernel, [(x.shape, x.dtype)], x, limit=2, flops=10**9)[0]


def concat_kernel(*refs):
    out = refs[-1]
    out[...] = jnp.concatenate([r[...].astype(F32) for r in refs[:-1]], axis=0).astype(BF16)


def stack(parts):
    if len(parts) == 1:
        return parts[0]
    rows = sum(p.shape[0] for p in parts)
    return local_call(concat_kernel, [((rows, parts[0].shape[1]), BF16)], *parts)[0]


def softmax_columns(logits):
    weight = jnp.exp(logits - jnp.max(logits, axis=0, keepdims=True))
    return weight / jnp.sum(weight, axis=0, keepdims=True)


def logit_kernel(table, tokens, tokens_far, logits_out, stats):
    logits = jnp.concatenate(
        [
            product(table[...], tokens[...], 1, 1),
            product(table[...], tokens_far[...], 1, 1),
        ],
        axis=1,
    )
    logits_out[...] = logits
    top = jnp.max(logits, axis=0, keepdims=True)
    total = jnp.sum(jnp.exp(logits - top), axis=0, keepdims=True)
    row = lax.broadcasted_iota(jnp.int32, stats.shape, 0)
    stats[...] = jnp.where(row == 0, top, jnp.where(row == 1, total, 0.0))


def dispatch_kernel(logits, tokens, tokens_far, sums, stats):
    patches = tokens.shape[0]
    top = jnp.max(logits[...], axis=1, keepdims=True)
    weight = jnp.exp(logits[...] - top)
    stats[...] = packed([top, jnp.sum(weight, axis=1, keepdims=True)], stats.shape[0]).astype(BF16)
    weight = weight.astype(BF16)
    both = product(weight[:, :patches], tokens[...], 1, 0)
    both += product(weight[:, patches:], tokens_far[...], 1, 0)
    sums[...] = both.astype(BF16)


def as_here(rows_far):
    half = rows_far.shape[1] // 2
    return jnp.concatenate([rows_far[:, half:], rows_far[:, :half]], axis=1)


def combine_weights(logits, rows, rows_far):
    other = as_here(rows_far)
    top = jnp.maximum(rows[:1], other[:1])
    total = rows[1:2] * jnp.exp(rows[:1] - top) + other[1:2] * jnp.exp(other[:1] - top)
    return jnp.exp(logits[...] - top) / total


def combine_kernel(logits, rows, rows_far, out_grad, out_far, sums, stats, *outs):
    patches, width = out_grad.shape
    combine = combine_weights(logits, rows, rows_far).astype(BF16)
    grads = product(combine[:, :patches], out_grad[...], 1, 0)
    grads += product(combine[:, patches:], out_far[...], 1, 0)
    count = outs[0].shape[0]
    for k, out in enumerate(outs):
        part = slice(k * count, (k + 1) * count)
        out[:, :width] = sums[part].astype(BF16)
        out[:, width : 2 * width] = grads[part].astype(BF16)
        out[:, 2 * width :] = stats[part]


def merged(refs, width):
    stats = [unpacked(r[:, 2 * width :].astype(F32), 2) for r in refs]
    top = stats[0][0]
    for other, _ in stats[1:]:
        top = jnp.maximum(top, other)
    scales = [jnp.exp(t - top) for t, _ in stats]
    total = sum(s * l for s, (_, l) in zip(scales, stats))
    sums = sum(s * r[:, :width].astype(F32) for s, r in zip(scales, refs))
    grads = sum(r[:, width : 2 * width].astype(F32) for r in refs)
    return sums, grads, top, total


def merge_kernel(count, unread, width, *refs):
    sums, grads, top, total = merged(refs[:count], width)
    outs = refs[count + unread :]
    rows = outs[0].shape[0]
    stats = packed([top, total], sums.shape[0])
    for k, out in enumerate(outs):
        part = slice(k * rows, (k + 1) * rows)
        out[:, :width] = sums[part].astype(BF16)
        out[:, width : 2 * width] = grads[part].astype(BF16)
        out[:, 2 * width :] = stats[part].astype(BF16)


def merge(parts, width, pieces, *after):
    rows, columns = parts[0].shape
    return local_call(
        partial(merge_kernel, len(parts), len(after), width),
        [((rows // pieces, columns), BF16)] * pieces,
        *parts,
        *after,
    )


def flip_kernel(index, weight, after, out):
    out[...] = weight[index].T


def flip_whole_kernel(x, out):
    out[...] = x[...].T


def flipped_whole(x):
    shape = (x.shape[1], x.shape[0])
    return local_call(flip_whole_kernel, [(shape, BF16)], x, flops=3 * 10**8)[0]


def flipped(weights, after):
    experts, rows, columns = weights.shape
    return [
        local_call(
            partial(flip_kernel, e), [((columns, rows), BF16)], weights, after, flops=10**9
        )[0]
        for e in range(experts)
    ]


def gelu_and_slope(v):
    root = math.sqrt(2.0 / math.pi)
    t = jnp.tanh(root * (v + 0.044715 * (v * v * v)))
    slope = 0.5 * (1.0 + t) + 0.5 * v * (1.0 - t * t) * (root * (1.0 + 3 * 0.044715 * (v * v)))
    return 0.5 * v * (1.0 + t), slope


def expert_kernel(count, width, *refs):
    parts = refs[:count]
    weight_in, weight_out = refs[count : count + 2]
    experts, _, units = weight_in.shape
    flips = refs[count + 2 : count + 2 + 2 * experts]
    in_flipped, out_flipped = flips[:experts], flips[experts:]
    both, slot_sum, stats = refs[count + 2 + 2 * experts :]
    sums, grads, top, total = merged(parts, width)
    stats[...] = packed([top, total], stats.shape[0])
    sums = sums / total
    slot_sum[...] = sums
    slot_in, grad_out = sums.astype(BF16), grads.astype(BF16)
    rows = sums.shape[0]
    step = min(units, 512)
    row = lax.broadcasted_iota(jnp.int32, (rows, step), 0)
    out_part = jnp.zeros((rows, width), F32)
    in_part = jnp.zeros((rows, width), F32)
    for e in range(experts):
        own = (row >= e * (rows // experts)) & (row < (e + 1) * (rows // experts))
        for c in range(units // step):
            at = slice(c * step, (c + 1) * step)
            pre_act = product(slot_in, weight_in[e, :, at], 1, 0)
            hid_grad = product(grad_out, out_flipped[e][:, at], 1, 0)
            act, slope = gelu_and_slope(pre_act)
            hidden = jnp.where(own, act, 0.0).astype(BF16)
            act_grad = jnp.where(own, hid_grad * slope, 0.0).astype(BF16)
            out_part += product(hidden, weight_out[e, at, :], 1, 0)
            in_part += product(act_grad, in_flipped[e][at, :], 1, 0)
    both[:, :width] = out_part.astype(BF16)
    both[:, width:] = in_part.astype(BF16)


def sum_kernel(count, *refs):
    total = sum(r[...].astype(F32) for r in refs[:count])
    outs = refs[count:]
    rows = outs[0].shape[0]
    for k, out in enumerate(outs):
        out[...] = total[k * rows : (k + 1) * rows].astype(out.dtype)


def sum_of(parts, pieces, dtype):
    rows, columns = parts[0].shape
    return local_call(
        partial(sum_kernel, len(parts)), [((rows // pieces, columns), dtype)] * pieces, *parts
    )


def centre_kernel(count, width, *refs):
    parts = refs[:count]
    slot_sum, stats, out = refs[count:]
    total = sum(r[...].astype(F32) for r in parts).astype(BF16)
    grad_in = total[:, width:].astype(F32)
    centre = jnp.sum(slot_sum[...] * grad_in, axis=1, keepdims=True)
    top, denominator = unpacked(stats[...], 2)
    out[:, : 2 * width] = total
    out[:, 2 * width :] = packed([centre, top, denominator], stats.shape[0]).astype(BF16)


def grad_kernel(
    near,
    logits,
    rows,
    rows_far,
    tokens_flipped,
    tokens_far,
    out_grad_flipped,
    out_far,
    direct,
    combine_out,
    dispatch_out,
    mean,
):
    width = tokens_flipped.shape[0]

    def against(columns, flipped_here, far):
        left = near[:, columns]
        return jnp.concatenate(
            [product(left, flipped_here[...], 1, 0), product(left, far[...], 1, 0)], axis=1
        )

    comb_grad = against(slice(0, width), out_grad_flipped, out_far)
    disp_grad = against(slice(width, 2 * width), tokens_flipped, tokens_far)
    centre, top, total = unpacked(near[:, 2 * width :].astype(F32), 3)
    dispatch = jnp.exp(logits[...] - top) / total
    combine = combine_weights(logits, rows, rows_far)
    weighted = combine * comb_grad
    direct[...] = dispatch * (disp_grad - centre) + weighted
    combine_out[...] = combine
    dispatch_out[...] = dispatch
    row = lax.broadcasted_iota(jnp.int32, mean.shape, 0)
    mean[...] = jnp.where(row == 0, jnp.sum(weighted, axis=0, keepdims=True), 0.0)


def block_kernel(
    order,
    direct,
    combine,
    dispatch,
    mean,
    mean_far,
    tokens,
    tokens_far,
    weights,
    weights_sent,
    blocks,
):
    patches, width = tokens.shape
    half = direct.shape[0]
    comb_mean = mean[:1] + as_here(mean_far)[:1]
    logit_grad = direct[...] - combine[...] * comb_mean
    logit_b = logit_grad.astype(BF16)
    part = product(logit_b[:, :patches], tokens[...], 1, 0)
    part += product(logit_b[:, patches:], tokens_far[...], 1, 0)
    part = part.astype(BF16)
    for out, at in ((weights, slice(0, patches)), (weights_sent, slice(patches, 2 * patches))):
        out[:half] = dispatch[:, at].astype(BF16)
        out[half:] = logit_b[:, at]
    chip = lax.axis_index("exp") // 2
    n_seq, n_chips = lax.axis_size("seq"), lax.axis_size("exp") // 2
    _, rows, share = blocks.shape
    for k, mask in enumerate(order):
        for s in range(n_seq):
            blocks[s * n_chips + (chip ^ mask)] = part[
                k * rows : (k + 1) * rows, s * share : (s + 1) * share
            ]


def grad_part_kernel(near, after, out):
    width = out.shape[1]
    out[...] = near[:, width : 2 * width]


def copy_kernel(x, after, out):
    out[...] = x[...]


def patch_kernel(weights, weights_far, near, table, grad_far, table_far, out):
    width = out.shape[1]
    left = jnp.concatenate([weights[...], weights_far[...]], axis=0)
    rows = jnp.concatenate(
        [near[:, width : 2 * width], table[...], grad_far[...], table_far[...]], axis=0
    )
    out[...] = product(left, rows, 0, 0).astype(BF16)


def shards(tokens, slot_embed, expert_in, expert_out, out_grad):
    width = tokens.shape[1]
    patches = tokens.shape[0]
    own = slot_embed.shape[1]
    n_exp, n_seq = lax.axis_size("exp"), lax.axis_size("seq")
    slots = own * n_exp
    half = slots // 2
    columns = 2 * width + LANES
    chip_groups = groups(n_exp, 2)
    seq_groups = groups(n_seq, 1)

    def gathered_over_chips(x, here):
        for masks in reversed(chip_groups):
            x = here = stack([here] + to_all(x, "exp", masks))
        return x

    table_near = gathered_over_chips(slot_embed.T, loaded(slot_embed.T))
    tokens_far, out_far = swap(tokens, "exp", 1), swap(out_grad, "exp", 1)

    tokens_flipped, out_grad_flipped = flipped_whole(tokens), flipped_whole(out_grad)
    logits, rows = local_call(
        logit_kernel,
        [((half, 2 * patches), F32), ((8, 2 * patches), F32)],
        table_near,
        tokens,
        tokens_far,
    )
    sums, stats = local_call(
        dispatch_kernel,
        [((half, width), BF16), ((half, LANES), BF16)],
        logits,
        tokens,
        tokens_far,
        flops=10**9,
    )
    pieces_first = len(chip_groups[0]) + 1
    rows_far = swap(rows, "exp", 1)
    pieces = local_call(
        combine_kernel,
        [((half // pieces_first, columns), BF16)] * pieces_first,
        logits,
        rows,
        rows_far,
        out_grad,
        out_far,
        sums,
        stats,
        limit=12,
    )
    for k, masks in enumerate(chip_groups):
        if k:
            pieces = merge(parts, width, len(masks) + 1)
        parts = [pieces[0]] + swaps(pieces[1:], "exp", masks)
    own_piece = pieces[0]
    for masks in seq_groups:
        (x,) = merge(parts, width, 1)
        parts = [x] + to_all(x, "seq", masks)
    own_sum = x

    both, slot_sum, stats = local_call(
        partial(expert_kernel, len(parts), width),
        [((own, 2 * width), BF16), ((own, width), F32), ((own, LANES), F32)],
        *parts,
        expert_in,
        expert_out,
        *flipped(expert_in, own_sum),
        *flipped(expert_out, own_piece),
        limit=16,
    )
    parts = [both]
    for k, masks in enumerate(seq_groups):
        if k:
            parts = list(sum_of(parts, 1, BF16))
        parts = parts + to_all(parts[0], "seq", masks)
    (packet,) = local_call(
        partial(centre_kernel, len(parts), width),
        [((own, columns), BF16)],
        *parts,
        slot_sum,
        stats,
    )
    (table_sent,) = local_call(
        copy_kernel, [((half, width), BF16)], table_near, packet, flops=10**8
    )
    table_far = swap(table_sent, "exp", 1)
    near = gathered_over_chips(packet, packet)
    direct, combine, dispatch, mean = local_call(
        grad_kernel,
        [((half, 2 * patches), F32)] * 3 + [((8, 2 * patches), F32)],
        near,
        logits,
        rows,
        rows_far,
        tokens_flipped,
        flipped_whole(tokens_far),
        out_grad_flipped,
        flipped_whole(out_far),
        limit=12,
    )
    order = [0]
    for masks in reversed(chip_groups):
        order = [r ^ (mask // 2) for mask in (0, *masks) for r in order]
    (grad_sent,) = local_call(
        grad_part_kernel, [((half, width), BF16)], near, mean, flops=10**8
    )
    weights, weights_sent, blocks = local_call(
        partial(block_kernel, order),
        [((2 * half, patches), BF16)] * 2
        + [((n_seq * n_exp // 2, own, width // n_seq), BF16)],
        direct,
        combine,
        dispatch,
        mean,
        swap(mean, "exp", 1),
        tokens,
        tokens_far,
        limit=12,
    )
    (tok_grad,) = local_call(
        patch_kernel,
        [((patches, width), BF16)],
        weights,
        swap(weights_sent, "exp", 1),
        near,
        table_near,
        swap(grad_sent, "exp", 1),
        table_far,
        limit=12,
        to_hbm=(0,),
    )
    same_core = [
        [s * n_exp + 2 * chip + core for s in range(n_seq) for chip in range(n_exp // 2)]
        for core in range(2)
    ]
    part = lax.all_to_all(
        blocks, ("seq", "exp"), 0, 0, tiled=True, axis_index_groups=same_core
    )
    part = jnp.sum(part.astype(F32), axis=0)
    return (tok_grad, part.T)


def solution(mesh):
    placed = (
        P(("seq", "exp"), None),
        P(None, "exp"),
        P("exp", None, "seq"),
        P("exp", "seq", None),
        P(("seq", "exp"), None),
    )
    return jax.shard_map(
        shards,
        mesh=mesh,
        in_specs=placed,
        out_specs=(P(("seq", "exp"), None), P("seq", "exp")),
        check_vma=False,
    )
```

```python
from functools import partial
import math

import jax
import jax.numpy as jnp
from jax import lax
from jax.experimental import pallas as pl
from jax.experimental.pallas import tpu as pltpu
from jax.sharding import PartitionSpec as P

LANES = 128
F32 = jnp.float32
BF16 = jnp.bfloat16
MIB = 1 << 20


def swap(x, axis, mask):
    return lax.ppermute(x, axis, [(k, k ^ mask) for k in range(lax.axis_size(axis))])


def swaps(parts, axis, masks):
    return [swap(x, axis, mask) for x, mask in zip(parts, masks)]


def to_all(x, axis, masks):
    return swaps([x] * len(masks), axis, masks)


def groups(n, first):
    bits = [1 << k for k in range(n.bit_length() - 1) if 1 << k >= first]
    return [
        [pair[1], sum(pair), pair[0]] if first > 1 else [sum(pair), pair[1], pair[0]]
        if len(pair) == 2
        else [pair[0]]
        for pair in (bits[k : k + 2] for k in range(0, len(bits), 2))
    ]


def in_vmem(x):
    return pltpu.with_memory_space_constraint(x, pltpu.VMEM)


def local_call(body, outs, *operands, limit=8, to_hbm=(), loose=(), flops=10**10):
    return pl.pallas_call(
        body,
        out_shape=tuple(
            jax.ShapeDtypeStruct(s, d) if k in to_hbm else pltpu.VMEM(s, d)
            for k, (s, d) in enumerate(outs)
        ),
        in_specs=[pl.BlockSpec(memory_space=pltpu.VMEM)] * len(operands),
        out_specs=tuple(pl.BlockSpec(memory_space=pltpu.VMEM) for _ in outs),
        compiler_params=pltpu.CompilerParams(vmem_limit_bytes=limit * MIB),
        cost_estimate=pl.CostEstimate(flops=flops, bytes_accessed=4 * MIB, transcendentals=0),
    )(*[in_vmem(x) for x in operands])


def product(left, right, over_left, over_right):
    return lax.dot_general(
        left, right, (((over_left,), (over_right,)), ((), ())), preferred_element_type=F32
    )


def rounded(x):
    return x.astype(BF16).astype(F32)


def packed(columns, rows):
    lane = lax.broadcasted_iota(jnp.int32, (rows, LANES), 1)
    out = jnp.zeros((rows, LANES), F32)
    for k, x in enumerate(columns):
        high = rounded(x)
        mid = rounded(x - high)
        for j, piece in enumerate((high, mid, x - high - mid)):
            out = jnp.where(lane == 3 * k + j, piece, out)
    return out


def unpacked(block, count):
    lane = lax.broadcasted_iota(jnp.int32, block.shape, 1)
    return [
        jnp.sum(
            jnp.where((lane >= 3 * k) & (lane < 3 * k + 3), block, 0.0), axis=1, keepdims=True
        )
        for k in range(count)
    ]


def plain_copy_kernel(x, out):
    out[...] = x[...]


def loaded(x):
    return local_call(plain_copy_kernel, [(x.shape, x.dtype)], x, limit=2, flops=10**9)[0]


def concat_kernel(*refs):
    out = refs[-1]
    out[...] = jnp.concatenate([r[...].astype(F32) for r in refs[:-1]], axis=0).astype(BF16)


def stack(parts):
    if len(parts) == 1:
        return parts[0]
    rows = sum(p.shape[0] for p in parts)
    return local_call(concat_kernel, [((rows, parts[0].shape[1]), BF16)], *parts)[0]


def softmax_columns(logits):
    weight = jnp.exp(logits - jnp.max(logits, axis=0, keepdims=True))
    return weight / jnp.sum(weight, axis=0, keepdims=True)


def logit_kernel(table, tokens, tokens_far, logits_out, stats):
    logits = jnp.concatenate(
        [
            product(table[...], tokens[...], 1, 1),
            product(table[...], tokens_far[...], 1, 1),
        ],
        axis=1,
    )
    logits_out[...] = logits
    top = jnp.max(logits, axis=0, keepdims=True)
    total = jnp.sum(jnp.exp(logits - top), axis=0, keepdims=True)
    row = lax.broadcasted_iota(jnp.int32, stats.shape, 0)
    stats[...] = jnp.where(row == 0, top, jnp.where(row == 1, total, 0.0))


def dispatch_kernel(logits, tokens, tokens_far, sums, stats):
    patches = tokens.shape[0]
    top = jnp.max(logits[...], axis=1, keepdims=True)
    weight = jnp.exp(logits[...] - top)
    stats[...] = packed([top, jnp.sum(weight, axis=1, keepdims=True)], stats.shape[0]).astype(BF16)
    weight = weight.astype(BF16)
    both = product(weight[:, :patches], tokens[...], 1, 0)
    both += product(weight[:, patches:], tokens_far[...], 1, 0)
    sums[...] = both.astype(BF16)


def as_here(rows_far):
    half = rows_far.shape[1] // 2
    return jnp.concatenate([rows_far[:, half:], rows_far[:, :half]], axis=1)


def combine_weights(logits, rows, rows_far):
    other = as_here(rows_far)
    top = jnp.maximum(rows[:1], other[:1])
    total = rows[1:2] * jnp.exp(rows[:1] - top) + other[1:2] * jnp.exp(other[:1] - top)
    return jnp.exp(logits[...] - top) / total


def combine_kernel(logits, rows, rows_far, out_grad, out_far, sums, stats, *outs):
    patches, width = out_grad.shape
    combine = combine_weights(logits, rows, rows_far).astype(BF16)
    grads = product(combine[:, :patches], out_grad[...], 1, 0)
    grads += product(combine[:, patches:], out_far[...], 1, 0)
    count = outs[0].shape[0]
    for k, out in enumerate(outs):
        part = slice(k * count, (k + 1) * count)
        out[:, :width] = sums[part].astype(BF16)
        out[:, width : 2 * width] = grads[part].astype(BF16)
        out[:, 2 * width :] = stats[part]


def merged(refs, width):
    stats = [unpacked(r[:, 2 * width :].astype(F32), 2) for r in refs]
    top = stats[0][0]
    for other, _ in stats[1:]:
        top = jnp.maximum(top, other)
    scales = [jnp.exp(t - top) for t, _ in stats]
    total = sum(s * l for s, (_, l) in zip(scales, stats))
    sums = sum(s * r[:, :width].astype(F32) for s, r in zip(scales, refs))
    grads = sum(r[:, width : 2 * width].astype(F32) for r in refs)
    return sums, grads, top, total


def merge_kernel(count, unread, width, *refs):
    sums, grads, top, total = merged(refs[:count], width)
    outs = refs[count + unread :]
    rows = outs[0].shape[0]
    stats = packed([top, total], sums.shape[0])
    for k, out in enumerate(outs):
        part = slice(k * rows, (k + 1) * rows)
        out[:, :width] = sums[part].astype(BF16)
        out[:, width : 2 * width] = grads[part].astype(BF16)
        out[:, 2 * width :] = stats[part].astype(BF16)


def merge(parts, width, pieces, *after):
    rows, columns = parts[0].shape
    return local_call(
        partial(merge_kernel, len(parts), len(after), width),
        [((rows // pieces, columns), BF16)] * pieces,
        *parts,
        *after,
    )


def flip_kernel(index, weight, after, out):
    out[...] = weight[index].T


def flip_whole_kernel(x, out):
    out[...] = x[...].T


def flipped_whole(x):
    shape = (x.shape[1], x.shape[0])
    return local_call(flip_whole_kernel, [(shape, BF16)], x, flops=3 * 10**8)[0]


def flipped(weights, after):
    experts, rows, columns = weights.shape
    return [
        local_call(
            partial(flip_kernel, e), [((columns, rows), BF16)], weights, after, flops=10**9
        )[0]
        for e in range(experts)
    ]


def gelu_and_slope(v):
    root = math.sqrt(2.0 / math.pi)
    t = jnp.tanh(root * (v + 0.044715 * (v * v * v)))
    slope = 0.5 * (1.0 + t) + 0.5 * v * (1.0 - t * t) * (root * (1.0 + 3 * 0.044715 * (v * v)))
    return 0.5 * v * (1.0 + t), slope


def expert_kernel(count, width, *refs):
    parts = refs[:count]
    weight_in, weight_out = refs[count : count + 2]
    experts, _, units = weight_in.shape
    flips = refs[count + 2 : count + 2 + 2 * experts]
    in_flipped, out_flipped = flips[:experts], flips[experts:]
    both, slot_sum, stats = refs[count + 2 + 2 * experts :]
    sums, grads, top, total = merged(parts, width)
    stats[...] = packed([top, total], stats.shape[0])
    sums = sums / total
    slot_sum[...] = sums
    slot_in, grad_out = sums.astype(BF16), grads.astype(BF16)
    rows = sums.shape[0]
    step = min(units, 512)
    row = lax.broadcasted_iota(jnp.int32, (rows, step), 0)
    out_part = jnp.zeros((rows, width), F32)
    in_part = jnp.zeros((rows, width), F32)
    for e in range(experts):
        own = (row >= e * (rows // experts)) & (row < (e + 1) * (rows // experts))
        for c in range(units // step):
            at = slice(c * step, (c + 1) * step)
            pre_act = product(slot_in, weight_in[e, :, at], 1, 0)
            hid_grad = product(grad_out, out_flipped[e][:, at], 1, 0)
            act, slope = gelu_and_slope(pre_act)
            hidden = jnp.where(own, act, 0.0).astype(BF16)
            act_grad = jnp.where(own, hid_grad * slope, 0.0).astype(BF16)
            out_part += product(hidden, weight_out[e, at, :], 1, 0)
            in_part += product(act_grad, in_flipped[e][at, :], 1, 0)
    both[:, :width] = out_part.astype(BF16)
    both[:, width:] = in_part.astype(BF16)


def sum_kernel(count, *refs):
    total = sum(r[...].astype(F32) for r in refs[:count])
    outs = refs[count:]
    rows = outs[0].shape[0]
    for k, out in enumerate(outs):
        out[...] = total[k * rows : (k + 1) * rows].astype(out.dtype)


def sum_of(parts, pieces, dtype):
    rows, columns = parts[0].shape
    return local_call(
        partial(sum_kernel, len(parts)), [((rows // pieces, columns), dtype)] * pieces, *parts
    )


def centre_kernel(count, width, *refs):
    parts = refs[:count]
    slot_sum, stats, out = refs[count:]
    total = sum(r[...].astype(F32) for r in parts).astype(BF16)
    grad_in = total[:, width:].astype(F32)
    centre = jnp.sum(slot_sum[...] * grad_in, axis=1, keepdims=True)
    top, denominator = unpacked(stats[...], 2)
    out[:, : 2 * width] = total
    out[:, 2 * width :] = packed([centre, top, denominator], stats.shape[0]).astype(BF16)


def grad_kernel(
    near,
    logits,
    rows,
    rows_far,
    tokens_flipped,
    tokens_far,
    out_grad_flipped,
    out_far,
    direct,
    combine_out,
    dispatch_out,
    mean,
):
    width = tokens_flipped.shape[0]

    def against(columns, flipped_here, far):
        left = near[:, columns]
        return jnp.concatenate(
            [product(left, flipped_here[...], 1, 0), product(left, far[...], 1, 0)], axis=1
        )

    comb_grad = against(slice(0, width), out_grad_flipped, out_far)
    disp_grad = against(slice(width, 2 * width), tokens_flipped, tokens_far)
    centre, top, total = unpacked(near[:, 2 * width :].astype(F32), 3)
    dispatch = jnp.exp(logits[...] - top) / total
    combine = combine_weights(logits, rows, rows_far)
    weighted = combine * comb_grad
    direct[...] = dispatch * (disp_grad - centre) + weighted
    combine_out[...] = combine
    dispatch_out[...] = dispatch
    row = lax.broadcasted_iota(jnp.int32, mean.shape, 0)
    mean[...] = jnp.where(row == 0, jnp.sum(weighted, axis=0, keepdims=True), 0.0)


def block_kernel(
    order,
    direct,
    combine,
    dispatch,
    mean,
    mean_far,
    tokens,
    tokens_far,
    weights,
    weights_sent,
    blocks,
):
    patches, width = tokens.shape
    half = direct.shape[0]
    comb_mean = mean[:1] + as_here(mean_far)[:1]
    logit_grad = direct[...] - combine[...] * comb_mean
    logit_b = logit_grad.astype(BF16)
    part = product(logit_b[:, :patches], tokens[...], 1, 0)
    part += product(logit_b[:, patches:], tokens_far[...], 1, 0)
    part = part.astype(BF16)
    for out, at in ((weights, slice(0, patches)), (weights_sent, slice(patches, 2 * patches))):
        out[:half] = dispatch[:, at].astype(BF16)
        out[half:] = logit_b[:, at]
    chip = lax.axis_index("exp") // 2
    n_seq, n_chips = lax.axis_size("seq"), lax.axis_size("exp") // 2
    _, rows, share = blocks.shape
    for k, mask in enumerate(order):
        for s in range(n_seq):
            blocks[s * n_chips + (chip ^ mask)] = part[
                k * rows : (k + 1) * rows, s * share : (s + 1) * share
            ]


def grad_part_kernel(near, after, out):
    width = out.shape[1]
    out[...] = near[:, width : 2 * width]


def block_sum_kernel(blocks, out):
    out[...] = sum(blocks[k].astype(F32) for k in range(blocks.shape[0]))


def copy_kernel(x, after, out):
    out[...] = x[...]


def patch_kernel(weights, weights_far, near, table, grad_far, table_far, out):
    width = out.shape[1]
    left = jnp.concatenate([weights[...], weights_far[...]], axis=0)
    rows = jnp.concatenate(
        [near[:, width : 2 * width], table[...], grad_far[...], table_far[...]], axis=0
    )
    out[...] = product(left, rows, 0, 0).astype(BF16)


def shards(tokens, slot_embed, expert_in, expert_out, out_grad):
    width = tokens.shape[1]
    patches = tokens.shape[0]
    own = slot_embed.shape[1]
    n_exp, n_seq = lax.axis_size("exp"), lax.axis_size("seq")
    slots = own * n_exp
    half = slots // 2
    columns = 2 * width + LANES
    chip_groups = groups(n_exp, 2)
    seq_groups = groups(n_seq, 1)

    def gathered_over_chips(x, here):
        for masks in reversed(chip_groups):
            x = here = stack([here] + to_all(x, "exp", masks))
        return x

    table_near = gathered_over_chips(slot_embed.T, loaded(slot_embed.T))
    tokens_far, out_far = swap(tokens, "exp", 1), swap(out_grad, "exp", 1)

    tokens_flipped, out_grad_flipped = flipped_whole(tokens), flipped_whole(out_grad)
    logits, rows = local_call(
        logit_kernel,
        [((half, 2 * patches), F32), ((8, 2 * patches), F32)],
        table_near,
        tokens,
        tokens_far,
    )
    sums, stats = local_call(
        dispatch_kernel,
        [((half, width), BF16), ((half, LANES), BF16)],
        logits,
        tokens,
        tokens_far,
        flops=10**9,
    )
    pieces_first = len(chip_groups[0]) + 1
    rows_far = swap(rows, "exp", 1)
    pieces = local_call(
        combine_kernel,
        [((half // pieces_first, columns), BF16)] * pieces_first,
        logits,
        rows,
        rows_far,
        out_grad,
        out_far,
        sums,
        stats,
        limit=12,
    )
    for k, masks in enumerate(chip_groups):
        if k:
            pieces = merge(parts, width, len(masks) + 1)
        parts = [pieces[0]] + swaps(pieces[1:], "exp", masks)
    own_piece = pieces[0]
    for masks in seq_groups:
        (x,) = merge(parts, width, 1)
        parts = [x] + to_all(x, "seq", masks)
    own_sum = x

    both, slot_sum, stats = local_call(
        partial(expert_kernel, len(parts), width),
        [((own, 2 * width), BF16), ((own, width), F32), ((own, LANES), F32)],
        *parts,
        expert_in,
        expert_out,
        *flipped(expert_in, own_sum),
        *flipped(expert_out, own_piece),
        limit=16,
    )
    parts = [both]
    for k, masks in enumerate(seq_groups):
        if k:
            parts = list(sum_of(parts, 1, BF16))
        parts = parts + to_all(parts[0], "seq", masks)
    (packet,) = local_call(
        partial(centre_kernel, len(parts), width),
        [((own, columns), BF16)],
        *parts,
        slot_sum,
        stats,
    )
    (table_sent,) = local_call(
        copy_kernel, [((half, width), BF16)], table_near, packet, flops=10**8
    )
    table_far = swap(table_sent, "exp", 1)
    near = gathered_over_chips(packet, packet)
    direct, combine, dispatch, mean = local_call(
        grad_kernel,
        [((half, 2 * patches), F32)] * 3 + [((8, 2 * patches), F32)],
        near,
        logits,
        rows,
        rows_far,
        tokens_flipped,
        flipped_whole(tokens_far),
        out_grad_flipped,
        flipped_whole(out_far),
        limit=12,
    )
    order = [0]
    for masks in reversed(chip_groups):
        order = [r ^ (mask // 2) for mask in (0, *masks) for r in order]
    (grad_sent,) = local_call(
        grad_part_kernel, [((half, width), BF16)], near, mean, flops=10**8
    )
    weights, weights_sent, blocks = local_call(
        partial(block_kernel, order),
        [((2 * half, patches), BF16)] * 2
        + [((n_seq * n_exp // 2, own, width // n_seq), BF16)],
        direct,
        combine,
        dispatch,
        mean,
        swap(mean, "exp", 1),
        tokens,
        tokens_far,
        limit=12,
    )
    (tok_grad,) = local_call(
        patch_kernel,
        [((patches, width), BF16)],
        weights,
        swap(weights_sent, "exp", 1),
        near,
        table_near,
        swap(grad_sent, "exp", 1),
        table_far,
        limit=12,
        to_hbm=(0,),
    )
    same_core = [
        [s * n_exp + 2 * chip + core for s in range(n_seq) for chip in range(n_exp // 2)]
        for core in range(2)
    ]
    part = lax.all_to_all(
        blocks, ("seq", "exp"), 0, 0, tiled=True, axis_index_groups=same_core
    )
    (part,) = local_call(
        block_sum_kernel, [(part.shape[1:], F32)], part, limit=4, to_hbm=(0,)
    )
    return (tok_grad, part.T)


def solution(mesh):
    placed = (
        P(("seq", "exp"), None),
        P(None, "exp"),
        P("exp", None, "seq"),
        P("exp", "seq", None),
        P(("seq", "exp"), None),
    )
    return jax.shard_map(
        shards,
        mesh=mesh,
        in_specs=placed,
        out_specs=(P(("seq", "exp"), None), P("seq", "exp")),
        check_vma=False,
    )
```
